256 devices in a mesh: gz: 64 (over x, y_lo, z), col: 2 (over core), af: 2 (over y_hi).
Axes of the slice: x: 4, y: 4 (y_hi: 2, y_lo: 2; y = y_hi * 2 + y_lo), z: 8, core: 2. Of those that a mesh axis runs over, the one named last changes fastest.
Arguments:
- volume: bfloat16 [128, 24, 24, 512], P('gz', 'af', None, 'col'), may hold values from -6 to 6
- kernel: bfloat16 [3, 3, 3, 512, 512], P(None, None, None, 'col', 'af'), may hold values from -0.0546875 to 0.0546875
- out_grad: bfloat16 [64, 12, 12, 512], P('gz', 'col', None, 'af'), may hold values from -6 to 6
Outputs:
- output: bfloat16 [64, 12, 12, 512], P('gz', 'col', None, 'af')
- volume_grad: bfloat16 [128, 24, 24, 512], P('gz', 'af', None, 'col')
- kernel_grad: bfloat16 [3, 3, 3, 512, 512], P(None, None, None, 'col', 'af')
The draws below stay inside these ranges and needn't reach their ends.
All inputs are finite; a program needn't handle non-finite values.
Results may differ from the reference program's by a relative error of at most 0.013.
Values may be sent and summed in bfloat16 or wider, within the bound.
A program may use at most 128 MiB of HBM per device.

```python
import jax
import jax.numpy as jnp
from jax import lax

CIN = 512
COUT = 512
NXY = 24
OXY = 12
NZ = 128
OZ = 64


def level_of(stream_key, shape, shards, least, top_value):
    level = 1.0
    for position, blocks in shards:
        steps = jax.random.uniform(jax.random.fold_in(jax.random.fold_in(stream_key, 6), position), (blocks,), jnp.float32, least / len(shards), top_value / len(shards))
        level = level * jnp.repeat(jnp.exp(steps), shape[position] // blocks).reshape((-1,) + (1,) * (len(shape) - 1 - position))
    return level


def gaussian(rng, shape, spread, reach, shards=(), dtype=jnp.bfloat16):
    values = spread * jax.random.normal(rng, shape, jnp.float32)
    if shards:
        values = values * level_of(rng, shape, shards, -0.22, 0.18)
    return jnp.clip(values, -reach, reach).astype(dtype)


def setup_inputs(seed: int = 0) -> dict:
    splits = jax.random.split(jax.random.key(seed), 4)
    return {
        "volume": gaussian(splits[0], (NZ, NXY, NXY, CIN), 1.0, 6.0, ((0, 64), (1, 2), (3, 2))),
        "kernel": gaussian(splits[1], (3, 3, 3, CIN, COUT), (27 * CIN) ** -0.5, 0.0546875, ((3, 2), (4, 2))),
        "out_grad": gaussian(splits[2], (OZ, OXY, OXY, COUT), 1.0, 6.0, ((0, 64), (1, 2), (3, 2))),
    }


def convolve(field, weights):
    return lax.conv_general_dilated(field, weights, (2, 2, 2), ((1, 0), (1, 0), (1, 0)), dimension_numbers=('NDHWC', 'DHWIO', 'NDHWC'), precision=lax.Precision.HIGHEST)

def reference(volume, kernel, out_grad):
    field = volume.astype(jnp.float32)[None]
    weights = kernel.astype(jnp.float32)
    result, pullback = jax.vjp(convolve, field, weights)
    field_grad, weight_grad = pullback(out_grad.astype(jnp.float32)[None])
    scale = 1.0 / jnp.sqrt(jnp.float32(OZ * OXY * OXY))
    output = result[0].astype(jnp.bfloat16)
    volume_grad = field_grad[0].astype(jnp.bfloat16)
    kernel_grad = (weight_grad * scale).astype(jnp.bfloat16)
    return (output, volume_grad, kernel_grad)
```

```python
import functools

import jax
import jax.numpy as jnp
from jax import lax
from jax.experimental import pallas as pl
from jax.experimental.pallas import tpu as pltpu
from jax.sharding import PartitionSpec as P

F32 = jnp.float32
BF16 = jnp.bfloat16
MESH = pl.DeviceIdType.MESH
NX, NY, NZ = 4, 2, 8
SHARD = 112
YZ = NY * NZ
BLOCK = SHARD * YZ
ROWS = BLOCK * NX
TAP_ROWS = 27 * 256


def rows_of(start, size):
    return pl.ds(pl.multiple_of(start, 16), size)


def body(
    v, k, og, out, vg, kg,
    k3, og3, vs, vin, halo, acc, vacc, oin, osend, vg_af, vg_gz, vin_af, vin_gz,
    ws, rx, s2, ry, full,
    local_sem, es, er, xs, xr, ys, yr, gs, gr, hs, hr,
):
    gz, col, af = lax.axis_index("gz"), lax.axis_index("col"), lax.axis_index("af")
    count = NX * YZ
    x, y, z = gz // YZ, (gz // NZ) % NY, gz % NZ
    up, down = lax.rem(gz + 1, count), lax.rem(gz + count - 1, count)

    def dev(g, c=col, a=af):
        return {"gz": g, "col": c, "af": a}

    def x_peer(d):
        return lax.rem(x + d, NX)

    def yz_peer(t):
        return lax.rem(y + t // NZ, NY) * NZ + lax.rem(z + t % NZ, NZ)

    def remote(src, dst, ss, rs, target):
        return pltpu.make_async_remote_copy(
            src_ref=src, dst_ref=dst, send_sem=ss, recv_sem=rs, device_id=target, device_id_type=MESH
        )

    barrier = pltpu.get_barrier_semaphore()

    def greet(target):
        pl.semaphore_signal(barrier, inc=1, device_id=target, device_id_type=MESH)

    greet(dev(gz, c=1 - col))
    greet(dev(gz, a=1 - af))
    for g in (up, down):
        greet(dev(g))
        greet(dev(g, a=1 - af))
    for d in range(1, NX):
        greet(dev(x_peer(d) * YZ + y * NZ + z))

    @pl.loop(1, YZ)
    def _(t):
        greet(dev(x * YZ + yz_peer(t)))

    loads = [
        pltpu.make_async_copy(k.at[:, c], k3.at[:, :, pl.ds(c * 256, 256)], local_sem.at[c])
        for c in range(3)
    ]
    for load in loads:
        load.start()

    og3[pl.ds(12, 1)] = jnp.zeros((1, 32, 768), BF16)
    og3[pl.ds(6 * col, 6)] = og[...]
    vs[...] = jnp.zeros(vs.shape, BF16)
    ws[pl.ds(TAP_ROWS, ROWS - TAP_ROWS)] = jnp.zeros((ROWS - TAP_ROWS, 256), BF16)
    pl.semaphore_wait(barrier, 1 + 1 + 4 + (NX - 1) + (YZ - 1))

    mine = pl.ds(6 * col, 6)
    cot = remote(og, og3.at[mine], es.at[0], er.at[0], dev(gz, c=1 - col))
    to_af = remote(v, vin, es.at[1], er.at[1], dev(gz, a=1 - af))
    top_own = remote(v.at[1], halo.at[0], es.at[2], er.at[2], dev(up))
    top_other = remote(v.at[1], halo.at[1], es.at[3], er.at[3], dev(up, a=1 - af))
    for copy in (cot, to_af, top_other, top_own):
        copy.start()

    own_pairs = pl.ds(1 + 6 * af, 6)
    other_pairs = pl.ds(7 - 6 * af, 6)
    for p in range(2):
        vs[p + 1, own_pairs, :, pl.ds(0, 24)] = v[p]

    for load in loads:
        load.wait()
    cot.wait()

    nt = (((1,), (1,)), ((), ()))

    @pl.loop(0, 3)
    def _(a):
        low = og3[pl.ds(0, 12)].reshape(384, 768)
        high = og3[pl.ds(1, 12)].reshape(384, 768)
        even = lax.dot_general(low, k3[a * 3 + 1], nt, preferred_element_type=F32)
        vacc[a, :, 0] = even.reshape(12, 32, 256)
        odd = lax.dot_general(low, k3[a * 3 + 2], nt, preferred_element_type=F32)
        odd = odd + lax.dot_general(high, k3[a * 3], nt, preferred_element_type=F32)
        vacc[a, :, 1] = odd.reshape(12, 32, 256)

    for p in range(2):
        vg_af[p] = vacc[p + 1, pl.ds(6 - 6 * af, 6), :, pl.ds(0, 24)].astype(BF16)
    vg_gz[0] = vacc[0, pl.ds(6 * af, 6), :, pl.ds(0, 24)].astype(BF16)
    vg_gz[1] = vacc[0, pl.ds(6 - 6 * af, 6), :, pl.ds(0, 24)].astype(BF16)
    back_af = remote(vg_af, vin_af, es.at[4], er.at[4], dev(gz, a=1 - af))
    back_own = remote(vg_gz.at[0], vin_gz.at[0], es.at[5], er.at[5], dev(down))
    back_other = remote(vg_gz.at[1], vin_gz.at[1], es.at[6], er.at[6], dev(down, a=1 - af))
    for copy in (back_af, back_own, back_other):
        copy.start()

    to_af.wait()
    for p in range(2):
        vs[p + 1, other_pairs, :, pl.ds(0, 24)] = vin[p]
    top_own.wait()
    top_other.wait()
    keep = jnp.where(gz > 0, 1.0, 0.0).astype(BF16)
    vs[0, own_pairs, :, pl.ds(0, 24)] = halo[0] * keep
    vs[0, other_pairs, :, pl.ds(0, 24)] = halo[1] * keep

    def planes(a, b):
        start, parity = (0, 1) if b == 0 else (1, b - 1)
        return vs[a, pl.ds(start, 12), parity].reshape(384, 256)

    tn = (((0,), (0,)), ((), ()))

    @pl.loop(0, 3)
    def _(a):
        field = og3[pl.ds(0, 12)].reshape(384, 768)
        for b in range(3):
            grad = lax.dot_general(planes(a, b), field, tn, preferred_element_type=F32).astype(BF16)
            for c in range(3):
                ws[rows_of((a * 9 + b * 3 + c) * 256, 256)] = grad[:, c * 256 : (c + 1) * 256]

    def x_send(d):
        target = x_peer(d)
        return remote(
            ws.at[rows_of(target * BLOCK, BLOCK)], rx.at[d - 1], xs.at[d - 1], xr.at[d - 1],
            dev(target * YZ + y * NZ + z),
        )

    for d in (2, 1, 3):
        x_send(d).start()

    acc[...] = jnp.zeros(acc.shape, F32)

    @pl.loop(0, 3)
    def _(a):
        for b in range(3):
            term = jnp.dot(planes(a, b), k3[a * 3 + b], preferred_element_type=F32)
            for n in range(6):
                acc[n, pl.ds(8, 384)] += term[:, n * 128 : (n + 1) * 128]

    def half(base):
        start = pl.multiple_of(base * 192, 8)
        total = None
        for c in range(3):
            term = jnp.concatenate(
                [
                    acc[c * 2 + lane, pl.ds(7 + c + start, 96, stride=2)]
                    for lane in range(2)
                ],
                axis=1,
            )
            if c == 0:
                place = lax.broadcasted_iota(jnp.int32, (96, 256), 0)
                term = jnp.where(place % 16 == 0, 0.0, term)
            total = term if total is None else total + term
        return total

    osend[...] = half(1 - col).astype(BF16).reshape(6, 16, 256)
    across = remote(osend, oin, es.at[7], er.at[7], dev(gz, c=1 - col))
    across.start()
    own_half = half(col)
    across.wait()
    out[...] = (own_half + oin[...].reshape(96, 256).astype(F32)).astype(BF16).reshape(6, 16, 256)

    for d in (1, 3, 2):
        x_send(d).wait()

    def y_send(t):
        peer = yz_peer(t)
        return remote(
            s2.at[rows_of(peer * SHARD, SHARD)], ry.at[t - 1], ys.at[t - 1], yr.at[t - 1],
            dev(x * YZ + peer),
        )

    def add_block(peer):
        local = rows_of(peer * SHARD, SHARD)
        total = ws[rows_of(x * BLOCK + peer * SHARD, SHARD)].astype(F32)
        for d in range(NX - 1):
            total = total + rx[d, local].astype(F32)
        return total

    @pl.loop(1, YZ)
    def _(t):
        peer = yz_peer(t)
        s2[rows_of(peer * SHARD, SHARD)] = add_block(peer).astype(BF16)
        y_send(t).start()

    back_af.wait()
    back_own.wait()
    back_other.wait()
    own = pl.ds(6 * af, 6)
    vg[0] = (vacc[1, own, :, pl.ds(0, 24)] + vin_af[0].astype(F32)).astype(BF16)
    above = vin_gz[0].astype(F32) + vin_gz[1].astype(F32)
    above = jnp.where(gz < count - 1, above, 0.0)
    vg[1] = (vacc[2, own, :, pl.ds(0, 24)] + vin_af[1].astype(F32) + above).astype(BF16)

    me = y * NZ + z
    for t in range(1, YZ):
        y_send(t).wait()
    total = add_block(me)
    for t in range(1, YZ):
        total = total + ry[t - 1].astype(F32)
    shard = x * BLOCK + me * SHARD
    full[rows_of(shard, SHARD)] = (total * (1.0 / jnp.sqrt(F32(9216)))).astype(BF16)

    def g_send(t):
        place = full.at[rows_of(shard, SHARD)]
        return remote(place, place, gs.at[t - 1], gr.at[t - 1], dev(x * YZ + yz_peer(t)))

    def g_wait(t):
        peer = lax.rem(y + NY - t // NZ, NY) * NZ + lax.rem(z + NZ - t % NZ, NZ)
        place = full.at[rows_of(x * BLOCK + peer * SHARD, SHARD)]
        remote(place, place, gs.at[t - 1], gr.at[t - 1], dev(x * YZ + peer)).wait_recv()

    def h_send(d):
        place = full.at[rows_of(x * BLOCK, BLOCK)]
        return remote(place, place, hs.at[d - 1], hr.at[d - 1], dev(x_peer(d) * YZ + me))

    def h_wait(d):
        source = lax.rem(x + NX - d, NX)
        place = full.at[rows_of(source * BLOCK, BLOCK)]
        remote(place, place, hs.at[d - 1], hr.at[d - 1], dev(source * YZ + me)).wait_recv()

    @pl.loop(1, YZ)
    def _(t):
        g_send(t).start()

    @pl.loop(1, YZ)
    def _(t):
        g_wait(t)

    for d in (2, 1, 3):
        h_send(d).start()
    for d in (1, 3, 2):
        h_wait(d)
    store = pltpu.make_async_copy(full.at[pl.ds(0, TAP_ROWS)], kg, local_sem.at[0])
    store.start()

    @pl.loop(1, YZ)
    def _(t):
        g_send(t).wait_send()

    for d in (1, 3, 2):
        h_send(d).wait_send()
    store.wait()


def upsample(og):
    even = lax.pad(og, jnp.zeros((), BF16), ((0, 0, 0), (0, 9, 1), (0, 0, 0)))
    odd = lax.pad(og, jnp.zeros((), BF16), ((0, 0, 0), (1, 8, 1), (0, 0, 0)))
    before = lax.pad(og[:, 1:], jnp.zeros((), BF16), ((0, 0, 0), (1, 10, 1), (0, 0, 0)))
    return jnp.concatenate([before, even, odd], axis=2)


def on_device(volume, kernel, out_grad):
    v = volume.reshape(2, 6, 2, 24, 256)
    og = upsample(out_grad.reshape(6, 12, 256))
    k = kernel.reshape(9, 3, 256, 256)
    vmem = pl.BlockSpec(memory_space=pltpu.VMEM)
    hbm = pl.BlockSpec(memory_space=pl.ANY)
    dma = pltpu.SemaphoreType.DMA
    out, vg, kg = pl.pallas_call(
        body,
        out_shape=(
            jax.ShapeDtypeStruct((6, 16, 256), BF16),
            jax.ShapeDtypeStruct((2, 6, 2, 24, 256), BF16),
            jax.ShapeDtypeStruct((TAP_ROWS, 256), BF16),
        ),
        in_specs=[vmem, hbm, vmem],
        out_specs=(vmem, vmem, hbm),
        scratch_shapes=[
            pltpu.VMEM((9, 256, 768), BF16),
            pltpu.VMEM((13, 32, 768), BF16),
            pltpu.VMEM((3, 13, 2, 32, 256), BF16),
            pltpu.VMEM((2, 6, 2, 24, 256), BF16),
            pltpu.VMEM((2, 6, 2, 24, 256), BF16),
            pltpu.VMEM((6, 392, 128), F32),
            pltpu.VMEM((3, 12, 2, 32, 256), F32),
            pltpu.VMEM((6, 16, 256), BF16),
            pltpu.VMEM((6, 16, 256), BF16),
            pltpu.VMEM((2, 6, 2, 24, 256), BF16),
            pltpu.VMEM((2, 6, 2, 24, 256), BF16),
            pltpu.VMEM((2, 6, 2, 24, 256), BF16),
            pltpu.VMEM((2, 6, 2, 24, 256), BF16),
            pltpu.VMEM((ROWS, 256), BF16),
            pltpu.VMEM((NX - 1, BLOCK, 256), BF16),
            pltpu.VMEM((BLOCK, 256), BF16),
            pltpu.VMEM((YZ - 1, SHARD, 256), BF16),
            pltpu.VMEM((ROWS, 256), BF16),
            dma((3,)),
            dma((8,)), dma((8,)),
            dma((NX - 1,)), dma((NX - 1,)),
            dma((YZ - 1,)), dma((YZ - 1,)),
            dma((YZ - 1,)), dma((YZ - 1,)),
            dma((NX - 1,)), dma((NX - 1,)),
        ],
        compiler_params=pltpu.CompilerParams(
            collective_id=0, has_side_effects=True, vmem_limit_bytes=56 * 2**20
        ),
    )(v, k, og)
    return (
        out[:, :12].reshape(1, 6, 12, 256),
        vg.reshape(2, 12, 24, 256),
        kg.reshape(3, 3, 3, 256, 256),
    )


def solution(mesh):
    in_specs = (
        P("gz", "af", None, "col"),
        P(None, None, None, "col", "af"),
        P("gz", "col", None, "af"),
    )
    out_specs = (
        P("gz", "col", None, "af"),
        P("gz", "af", None, "col"),
        P(None, None, None, "col", "af"),
    )
    return jax.shard_map(
        on_device, mesh=mesh, in_specs=in_specs, out_specs=out_specs, check_vma=False
    )
```

```python
import functools

import jax
import jax.numpy as jnp
from jax import lax
from jax.experimental import pallas as pl
from jax.experimental.pallas import tpu as pltpu
from jax.sharding import PartitionSpec as P

F32 = jnp.float32
BF16 = jnp.bfloat16
MESH = pl.DeviceIdType.MESH
NX, NY, NZ = 4, 2, 8
XY, YZ = NX * NY, NY * NZ
PART_A, PART_B = 64, 48
A_BLOCK, A_PIECE = PART_A * YZ, PART_A * NY
B_BASE, B_BLOCK, B_PIECE = A_BLOCK * NX, PART_B * XY, PART_B * NY
ROWS = B_BASE + B_BLOCK * NZ
TAP_ROWS = 27 * 256
FAR_FIRST = (4, 3, 5, 2, 6, 1, 7, 0)
NEAR_FIRST = (0, 1, 7, 2, 6, 3, 5, 4)


def rows_of(start, size):
    return pl.ds(pl.multiple_of(start, 16), size)


def body(
    v, k, og, out, vg, full,
    k3, up, og3, vs, vin, halo, acc, vacc, oin, osend, vg_af, vg_gz, vin_af, vin_gz,
    ws, rx, s2, ry, br, sb, bx,
    local_sem, es, er, axs, axr, ays, ayr, brs, brr, bxs, bxr,
    gays, gayr, gaxs, gaxr, gbxs, gbxr, gbrs, gbrr,
):
    gz, col, af = lax.axis_index("gz"), lax.axis_index("col"), lax.axis_index("af")
    count = XY * NZ
    x, y, z = gz // YZ, (gz // NZ) % NY, gz % NZ
    upper, lower = lax.rem(gz + 1, count), lax.rem(gz + count - 1, count)

    def dev(g, c=col, a=af):
        return {"gz": g, "col": c, "af": a}

    def at(dx=0, dy=0, dz=0):
        return (lax.rem(x + dx + NX, NX), lax.rem(y + dy + NY, NY), lax.rem(z + dz + NZ, NZ))

    def chip(place):
        return dev((place[0] * NY + place[1]) * NZ + place[2])

    def remote(src, dst, ss, rs, target):
        return pltpu.make_async_remote_copy(
            src_ref=src, dst_ref=dst, send_sem=ss, recv_sem=rs, device_id=target, device_id_type=MESH
        )

    barrier = pltpu.get_barrier_semaphore()

    def greet(target):
        pl.semaphore_signal(barrier, inc=1, device_id=target, device_id_type=MESH)

    greet(dev(gz, c=1 - col))
    greet(dev(gz, a=1 - af))
    for g in (upper, lower):
        greet(dev(g))
        greet(dev(g, a=1 - af))

    @pl.loop(1, YZ)
    def _(t):
        greet(chip(at(0, t % NY, t // NY)))

    @pl.loop(NY, XY)
    def _(t):
        greet(chip(at(t // NY, t % NY, 0)))

    loads = [
        pltpu.make_async_copy(k.at[:, c], k3.at[:, :, pl.ds(c * 256, 256)], local_sem.at[c])
        for c in range(3)
    ]
    for load in loads:
        load.start()

    mine = pl.ds(6 * col, 6)
    up[...] = jnp.zeros(up.shape, F32)
    for i in range(6):
        row = og[i].astype(F32)
        for n in range(2):
            up[n, pl.ds(8 + 32 * i, 12, stride=2)] = row[:, n * 128 : (n + 1) * 128]
    for c in range(3):
        for n in range(2):
            og3[mine, :, pl.ds(c * 256 + n * 128, 128)] = (
                up[n, pl.ds(9 - c, 192)].reshape(6, 32, 128).astype(BF16)
            )
    og3[pl.ds(12, 1)] = jnp.zeros((1, 32, 768), BF16)
    vs[...] = jnp.zeros(vs.shape, BF16)
    ws[pl.ds(TAP_ROWS, ROWS - TAP_ROWS)] = jnp.zeros((ROWS - TAP_ROWS, 256), BF16)
    pl.semaphore_wait(barrier, 1 + 1 + 4 + (YZ - 1) + (XY - NY))

    cot = remote(og3.at[mine], og3.at[mine], es.at[0], er.at[0], dev(gz, c=1 - col))
    to_af = remote(v, vin, es.at[1], er.at[1], dev(gz, a=1 - af))
    top_own = remote(v.at[1], halo.at[0], es.at[2], er.at[2], dev(upper))
    top_other = remote(v.at[1], halo.at[1], es.at[3], er.at[3], dev(upper, a=1 - af))
    for copy in (cot, to_af, top_other, top_own):
        copy.start()

    own_pairs = pl.ds(1 + 6 * af, 6)
    other_pairs = pl.ds(7 - 6 * af, 6)
    for p in range(2):
        vs[p + 1, own_pairs, :, pl.ds(0, 24)] = v[p]

    for load in loads:
        load.wait()
    cot.wait_send()
    other = pl.ds(6 - 6 * col, 6)
    remote(og3.at[other], og3.at[other], es.at[0], er.at[0], dev(gz, c=1 - col)).wait_recv()

    nt = (((1,), (1,)), ((), ()))

    @pl.loop(0, 3)
    def _(a):
        low = og3[pl.ds(0, 12)].reshape(384, 768)
        high = og3[pl.ds(1, 12)].reshape(384, 768)
        even = lax.dot_general(low, k3[a * 3 + 1], nt, preferred_element_type=F32)
        vacc[a, :, 0] = even.reshape(12, 32, 256)
        odd = lax.dot_general(low, k3[a * 3 + 2], nt, preferred_element_type=F32)
        odd = odd + lax.dot_general(high, k3[a * 3], nt, preferred_element_type=F32)
        vacc[a, :, 1] = odd.reshape(12, 32, 256)

    for p in range(2):
        vg_af[p] = vacc[p + 1, pl.ds(6 - 6 * af, 6), :, pl.ds(0, 24)].astype(BF16)
    vg_gz[0] = vacc[0, pl.ds(6 * af, 6), :, pl.ds(0, 24)].astype(BF16)
    vg_gz[1] = vacc[0, pl.ds(6 - 6 * af, 6), :, pl.ds(0, 24)].astype(BF16)
    back_af = remote(vg_af, vin_af, es.at[4], er.at[4], dev(gz, a=1 - af))
    back_own = remote(vg_gz.at[0], vin_gz.at[0], es.at[5], er.at[5], dev(lower))
    back_other = remote(vg_gz.at[1], vin_gz.at[1], es.at[6], er.at[6], dev(lower, a=1 - af))
    for copy in (back_af, back_own, back_other):
        copy.start()

    to_af.wait()
    for p in range(2):
        vs[p + 1, other_pairs, :, pl.ds(0, 24)] = vin[p]
    top_own.wait()
    top_other.wait()
    keep = jnp.where(gz > 0, 1.0, 0.0).astype(BF16)
    vs[0, own_pairs, :, pl.ds(0, 24)] = halo[0] * keep
    vs[0, other_pairs, :, pl.ds(0, 24)] = halo[1] * keep

    def planes(ab):
        b = ab % 3
        return vs[ab // 3, pl.ds(jnp.minimum(b, 1), 12), (b + 1) % 2].reshape(384, 256)

    tn = (((0,), (0,)), ((), ()))

    def weight(ab):
        field = og3[pl.ds(0, 12)].reshape(384, 768)
        grad = lax.dot_general(planes(ab), field, tn, preferred_element_type=F32).astype(BF16)
        for c in range(3):
            ws[rows_of((ab * 3 + c) * 256, 256)] = grad[:, c * 256 : (c + 1) * 256]

    def b_rows(owner, j):
        return rows_of(B_BASE + owner * B_BLOCK + j * B_PIECE, B_PIECE)

    def sign(way):
        return 1 if way == 0 else -1

    def lanes(way):
        return pl.ds(128 * way, 128)

    def ring(way, s, j):
        piece = rows_of(j * B_PIECE, B_PIECE)
        if s == 0:
            src = ws.at[b_rows(at(dz=4)[2], j), lanes(way)]
            dst = br.at[way, 0, piece, lanes(way)]
        else:
            src, dst = br.at[way, s - 1, piece], br.at[way, s, piece]
        return remote(src, dst, brs.at[way, s, j], brr.at[way, s, j], chip(at(dz=sign(way))))

    def near(dj):
        return lax.rem(x + dj, NX)

    def ax_send(d, dz):
        xt, zt = at(dx=d)[0], at(dz=dz)[2]
        return remote(
            ws.at[rows_of(xt * A_BLOCK + zt * A_PIECE, A_PIECE)], rx.at[d - 1, dz],
            axs.at[d - 1, dz], axr.at[d - 1, dz], chip(at(dx=d)),
        )

    def ay_send(dy, dz):
        slot = dz * NY + dy - 1
        yt = at(dy=dy)[1]
        return remote(
            s2.at[dz, rows_of(yt * PART_A, PART_A)], ry.at[slot], ays.at[slot], ayr.at[slot],
            chip(at(dy=dy, dz=dz)),
        )

    def bx_send(dx, dy):
        slot = dx * NY + dy - 1
        xt, yt, _ = at(dx, dy)
        return remote(
            sb.at[rows_of((xt * NY + yt) * PART_B, PART_B)], bx.at[slot], bxs.at[slot], bxr.at[slot],
            chip(at(dx, dy)),
        )

    @pl.loop(0, 4)
    def _(i):
        weight(8 - i)

    @pl.loop(0, NX)
    def _(dj):
        for way in range(2):
            ring(way, 0, near(dj)).start()

    @pl.loop(0, 5)
    def _(i):
        weight(4 - i)

    for dz in FAR_FIRST:
        for d in (2, 1, 3):
            ax_send(d, dz).start()

    acc[...] = jnp.zeros(acc.shape, F32)

    def forward(first):
        @pl.loop(first, first + 3)
        def _(ab):
            term = jnp.dot(planes(ab), k3[ab], preferred_element_type=F32)
            for n in range(6):
                acc[n, pl.ds(8, 384)] += term[:, n * 128 : (n + 1) * 128]

    def ring_step(s):
        @pl.loop(0, NX)
        def _(dj):
            j = near(dj)
            piece = rows_of(j * B_PIECE, B_PIECE)
            for way in range(2):
                ring(way, s, j).wait_recv()
                if s == 3:
                    continue
                own = ws[b_rows(at(dz=sign(way) * (3 - s))[2], j)].astype(F32)
                if s == 0:
                    half, rest = slice(128 * way, 128 * way + 128), slice(128 - 128 * way, 256 - 128 * way)
                    br[way, 0, piece, lanes(way)] = (
                        br[way, 0, piece, lanes(way)].astype(F32) + own[:, half]
                    ).astype(BF16)
                    br[way, 0, piece, lanes(1 - way)] = own[:, rest].astype(BF16)
                else:
                    br[way, s, piece] = (br[way, s, piece].astype(F32) + own).astype(BF16)
                ring(way, s + 1, j).start()
            if s == 3:
                total = ws[b_rows(z, j)].astype(F32)
                total = total + br[0, 3, piece].astype(F32) + br[1, 3, piece].astype(F32)
                sb[piece] = total.astype(BF16)
                bx_send(dj, 1).start()

                @pl.when(dj > 0)
                def _():
                    bx_send(dj, 0).start()

    def a_piece(dz):
        zt = at(dz=dz)[2]
        total = ws[rows_of(x * A_BLOCK + zt * A_PIECE, A_PIECE)].astype(F32)
        for d in range(1, NX):
            ax_send(d, dz).wait_recv()
            total = total + rx[d - 1, dz].astype(F32)
        s2[dz] = total.astype(BF16)
        for dy in range(NY):
            if dy or dz:
                ay_send(dy, dz).start()

    def half(base):
        start = pl.multiple_of(base * 192, 8)
        total = None
        for c in range(3):
            term = jnp.concatenate(
                [
                    acc[c * 2 + lane, pl.ds(7 + c + start, 96, stride=2)]
                    for lane in range(2)
                ],
                axis=1,
            )
            if c == 0:
                place = lax.broadcasted_iota(jnp.int32, (96, 256), 0)
                term = jnp.where(place % 16 == 0, 0.0, term)
            total = term if total is None else total + term
        return total

    across = remote(osend, oin, es.at[7], er.at[7], dev(gz, c=1 - col))
    forward(0)
    for s in range(4):
        ring_step(s)
        if s < 2:
            forward(3 + 3 * s)
        if s == 2:
            osend[...] = half(1 - col).astype(BF16).reshape(6, 16, 256)
            across.start()
        a_piece(FAR_FIRST[2 * s])
        a_piece(FAR_FIRST[2 * s + 1])

    scale = 1.0 / jnp.sqrt(F32(9216))
    total = sb[rows_of((x * NY + y) * PART_B, PART_B)].astype(F32)
    for slot in range(XY - 1):
        bx_send((slot + 1) // NY, (slot + 1) % NY).wait_recv()
        total = total + bx[slot].astype(F32)

    def a_shard(px, py, pz):
        return rows_of(px * A_BLOCK + pz * A_PIECE + py * PART_A, PART_A)

    def b_shard(px, py, pz):
        return rows_of(B_BASE + pz * B_BLOCK + (px * NY + py) * PART_B, PART_B)

    full[b_shard(x, y, z)] = (total * scale).astype(BF16)

    def gbx(dx, dy, source):
        slot = dx * NY + dy - 1
        place = full.at[b_shard(*source)]
        return remote(place, place, gbxs.at[slot], gbxr.at[slot], chip(at(dx, dy)))

    def gay(dy, dz, source):
        slot = dz * NY + dy - 1
        place = full.at[a_shard(*source)]
        return remote(place, place, gays.at[slot], gayr.at[slot], chip(at(dy=dy, dz=dz)))

    @pl.loop(1, XY)
    def _(t):
        gbx(t // NY, t % NY, (x, y, z)).start()

    total = s2[0, rows_of(y * PART_A, PART_A)].astype(F32)
    for dz in FAR_FIRST:
        for dy in range(NY):
            if dy or dz:
                ay_send(dy, dz).wait_recv()
                total = total + ry[dz * NY + dy - 1].astype(F32)
    full[a_shard(x, y, z)] = (total * scale).astype(BF16)

    for dz in NEAR_FIRST:
        for dy in range(NY):
            if dy or dz:
                gay(dy, dz, (x, y, z)).start()

    def gax(d, e, px):
        pz = at(dz=e)[2]
        place = full.at[rows_of(px * A_BLOCK + pz * A_PIECE, A_PIECE)]
        return remote(place, place, gaxs.at[d - 1, e], gaxr.at[d - 1, e], chip(at(dx=d)))

    def gring(way, s, j, arriving=False):
        pz = at(dz=-sign(way) * (s + 1 if arriving else s))[2]
        place = full.at[b_rows(pz, j)] if s < 3 else full.at[b_rows(pz, j), lanes(way)]
        return remote(place, place, gbrs.at[way, s, j], gbrr.at[way, s, j], chip(at(dz=sign(way))))

    def gather_piece(e):
        dz = (NZ - e) % NZ
        for dy in range(NY):
            if dy or dz:
                gay(dy, dz, at(0, -dy, -dz)).wait_recv()
        for d in (2, 1, 3):
            gax(d, e, x).start()

    @pl.loop(0, NX)
    def _(dj):
        j = near(dj)
        back = (NX - dj) % NX
        gbx(back, 1, at(dj, 1, 0)).wait_recv()

        @pl.when(dj > 0)
        def _():
            gbx(back, 0, at(dj, 0, 0)).wait_recv()

        for way in range(2):
            gring(way, 0, j).start()

    gather_piece(NEAR_FIRST[0])

    own_half = half(col)
    oin_copy = remote(osend, oin, es.at[7], er.at[7], dev(gz, c=1 - col))
    oin_copy.wait()
    out[...] = (own_half + oin[...].reshape(96, 256).astype(F32)).astype(BF16).reshape(6, 16, 256)
    back_af.wait()
    back_own.wait()
    back_other.wait()
    own = pl.ds(6 * af, 6)
    vg[0] = (vacc[1, own, :, pl.ds(0, 24)] + vin_af[0].astype(F32)).astype(BF16)
    above = vin_gz[0].astype(F32) + vin_gz[1].astype(F32)
    above = jnp.where(gz < count - 1, above, 0.0)
    vg[1] = (vacc[2, own, :, pl.ds(0, 24)] + vin_af[1].astype(F32) + above).astype(BF16)

    for s in range(4):
        for e in NEAR_FIRST[1 + 2 * s : 3 + 2 * s]:
            gather_piece(e)

        @pl.loop(0, NX)
        def _(dj):
            j = near(dj)
            for way in range(2):
                gring(way, s, j, True).wait_recv()
                if s < 3:
                    gring(way, s + 1, j).start()

    for e in NEAR_FIRST:
        for d in (2, 1, 3):
            gax(d, e, at(dx=-d)[0]).wait_recv()

    @pl.loop(0, NX)
    def _(dj):
        for way in range(2):
            for s in range(4):
                ring(way, s, near(dj)).wait_send()
                gring(way, s, near(dj)).wait_send()

    @pl.loop(0, NZ)
    def _(dz):
        for d in range(1, NX):
            ax_send(d, dz).wait_send()
            gax(d, dz, x).wait_send()

    @pl.loop(1, YZ)
    def _(t):
        ay_send(t % NY, t // NY).wait_send()
        gay(t % NY, t // NY, (x, y, z)).wait_send()

    @pl.loop(1, XY)
    def _(t):
        bx_send(t // NY, t % NY).wait_send()
        gbx(t // NY, t % NY, (x, y, z)).wait_send()


def on_device(volume, kernel, out_grad):
    v = volume.reshape(2, 6, 2, 24, 256)
    og = out_grad.reshape(6, 12, 256)
    k = kernel.reshape(9, 3, 256, 256)
    vmem = pl.BlockSpec(memory_space=pltpu.VMEM)
    hbm = pl.BlockSpec(memory_space=pltpu.HBM)
    dma = pltpu.SemaphoreType.DMA
    planes_shape = (2, 6, 2, 24, 256)

    def pair(*shape):
        return [dma(shape), dma(shape)]

    out, vg, kg = pl.pallas_call(
        body,
        out_shape=(
            jax.ShapeDtypeStruct((6, 16, 256), BF16),
            jax.ShapeDtypeStruct(planes_shape, BF16),
            jax.ShapeDtypeStruct((ROWS, 256), BF16),
        ),
        in_specs=[vmem, hbm, vmem],
        out_specs=(vmem, vmem, vmem),
        scratch_shapes=[
            pltpu.VMEM((9, 256, 768), BF16),
            pltpu.VMEM((2, 208, 128), F32),
            pltpu.VMEM((13, 32, 768), BF16),
            pltpu.VMEM((3, 13, 2, 32, 256), BF16),
            pltpu.VMEM(planes_shape, BF16),
            pltpu.VMEM(planes_shape, BF16),
            pltpu.VMEM((6, 392, 128), F32),
            pltpu.VMEM((3, 12, 2, 32, 256), F32),
            pltpu.VMEM((6, 16, 256), BF16),
            pltpu.VMEM((6, 16, 256), BF16),
            pltpu.VMEM(planes_shape, BF16),
            pltpu.VMEM(planes_shape, BF16),
            pltpu.VMEM(planes_shape, BF16),
            pltpu.VMEM(planes_shape, BF16),
            pltpu.VMEM((ROWS, 256), BF16),
            pltpu.VMEM((NX - 1, NZ, A_PIECE, 256), BF16),
            pltpu.VMEM((NZ, A_PIECE, 256), BF16),
            pltpu.VMEM((YZ - 1, PART_A, 256), BF16),
            pltpu.VMEM((2, 4, B_BLOCK, 256), BF16),
            pltpu.VMEM((B_BLOCK, 256), BF16),
            pltpu.VMEM((XY - 1, PART_B, 256), BF16),
            dma((3,)),
            *pair(8),
            *pair(NX - 1, NZ), *pair(YZ - 1), *pair(2, 4, NX), *pair(XY - 1),
            *pair(YZ - 1), *pair(NX - 1, NZ), *pair(XY - 1), *pair(2, 4, NX),
        ],
        compiler_params=pltpu.CompilerParams(
            collective_id=0, has_side_effects=True, vmem_limit_bytes=40 * 2**20
        ),
    )(v, k, og)
    return (
        out[:, :12].reshape(1, 6, 12, 256),
        vg.reshape(2, 12, 24, 256),
        kg[:TAP_ROWS].reshape(3, 3, 3, 256, 256),
    )


def solution(mesh):
    in_specs = (
        P("gz", "af", None, "col"),
        P(None, None, None, "col", "af"),
        P("gz", "col", None, "af"),
    )
    out_specs = (
        P("gz", "col", None, "af"),
        P("gz", "af", None, "col"),
        P(None, None, None, "col", "af"),
    )
    return jax.shard_map(
        on_device, mesh=mesh, in_specs=in_specs, out_specs=out_specs, check_vma=False
    )
```

```python
import functools

import jax
import jax.numpy as jnp
from jax import lax
from jax.experimental import pallas as pl
from jax.experimental.pallas import tpu as pltpu
from jax.sharding import PartitionSpec as P

F32 = jnp.float32
BF16 = jnp.bfloat16
MESH = pl.DeviceIdType.MESH
NX, NY, NZ = 4, 2, 8
XY, YZ = NX * NY, NY * NZ
PART_A, PART_B = 64, 48
A_BLOCK, A_PIECE = PART_A * YZ, PART_A * NY
B_BLOCK, B_PIECE = PART_B * XY, PART_B * NY
B_CHUNK = B_PIECE * NZ
A_BASE = B_BLOCK * NZ
ROWS = A_BASE + A_BLOCK * NX
FIRST_TAP = 256
FAR_FIRST = (4, 3, 5, 2, 6, 1, 7, 0)
NEAR_FIRST = (0, 1, 7, 2, 6, 3, 5, 4)


def rows_of(start, size):
    return pl.ds(pl.multiple_of(start, 16), size)


def body(
    v_hbm, k, og_hbm, out, vg, full,
    v, og, k3, up, og3, vs, vin, halo, acc, vacc, oin, osend, vg_af, vg_gz, vin_af, vin_gz,
    ws, rx, s2, ry, br, sb, bx,
    local_sem, es, er, axs, axr, ays, ayr, brs, brr, bxs, bxr,
    gazs, gazr, gaxs, gaxr, gbxs, gbxr, gbrs, gbrr,
):
    gz, col, af = lax.axis_index("gz"), lax.axis_index("col"), lax.axis_index("af")
    count = XY * NZ
    x, y, z = gz // YZ, (gz // NZ) % NY, gz % NZ
    upper, lower = lax.rem(gz + 1, count), lax.rem(gz + count - 1, count)

    def dev(g, c=col, a=af):
        return {"gz": g, "col": c, "af": a}

    def at(dx=0, dy=0, dz=0):
        return (lax.rem(x + dx + NX, NX), lax.rem(y + dy + NY, NY), lax.rem(z + dz + NZ, NZ))

    def chip(place):
        return dev((place[0] * NY + place[1]) * NZ + place[2])

    def remote(src, dst, ss, rs, target):
        return pltpu.make_async_remote_copy(
            src_ref=src, dst_ref=dst, send_sem=ss, recv_sem=rs, device_id=target, device_id_type=MESH
        )

    barrier = pltpu.get_barrier_semaphore()

    def greet(target):
        pl.semaphore_signal(barrier, inc=1, device_id=target, device_id_type=MESH)

    greet(dev(gz, c=1 - col))
    greet(dev(gz, a=1 - af))
    for g in (upper, lower):
        greet(dev(g))
        greet(dev(g, a=1 - af))

    @pl.loop(1, YZ)
    def _(t):
        greet(chip(at(0, t % NY, t // NY)))

    @pl.loop(NY, XY)
    def _(t):
        greet(chip(at(t // NY, t % NY, 0)))

    loads = [
        pltpu.make_async_copy(k.at[:, c], k3.at[:, :, pl.ds(c * 256, 256)], local_sem.at[c])
        for c in range(3)
    ]
    load_og = pltpu.make_async_copy(og_hbm, og, local_sem.at[3])
    load_v = pltpu.make_async_copy(v_hbm, v, local_sem.at[4])
    load_og.start()
    load_v.start()
    for load in loads:
        load.start()

    mine = pl.ds(6 * col, 6)
    up[...] = jnp.zeros(up.shape, F32)
    vs[...] = jnp.zeros(vs.shape, BF16)
    ws[pl.ds(0, FIRST_TAP)] = jnp.zeros((FIRST_TAP, 256), BF16)
    load_og.wait()
    for i in range(6):
        row = og[i].astype(F32)
        for n in range(2):
            up[n, pl.ds(8 + 32 * i, 12, stride=2)] = row[:, n * 128 : (n + 1) * 128]
    for c in range(3):
        for n in range(2):
            og3[mine, :, pl.ds(c * 256 + n * 128, 128)] = (
                up[n, pl.ds(9 - c, 192)].reshape(6, 32, 128).astype(BF16)
            )
    og3[pl.ds(12, 1)] = jnp.zeros((1, 32, 768), BF16)
    load_v.wait()
    pl.semaphore_wait(barrier, 1 + 1 + 4 + (YZ - 1) + (XY - NY))

    cot = remote(og3.at[mine], og3.at[mine], es.at[0], er.at[0], dev(gz, c=1 - col))
    to_af = [
        remote(v.at[p], vin.at[p], es.at[p + 1], er.at[p + 1], dev(gz, a=1 - af)) for p in range(2)
    ]
    top_own = remote(v.at[1], halo.at[0], es.at[8], er.at[8], dev(upper))
    top_other = remote(v.at[1], halo.at[1], es.at[3], er.at[3], dev(upper, a=1 - af))
    for copy in (cot, to_af[1], top_own, to_af[0], top_other):
        copy.start()

    own_pairs = pl.ds(1 + 6 * af, 6)
    other_pairs = pl.ds(7 - 6 * af, 6)
    for p in range(2):
        vs[p + 1, own_pairs, :, pl.ds(0, 24)] = v[p]

    for load in loads:
        load.wait()
    cot.wait_send()
    other = pl.ds(6 - 6 * col, 6)
    remote(og3.at[other], og3.at[other], es.at[0], er.at[0], dev(gz, c=1 - col)).wait_recv()

    nt = (((1,), (1,)), ((), ()))

    @pl.loop(0, 3)
    def _(a):
        low = og3[pl.ds(0, 12)].reshape(384, 768)
        high = og3[pl.ds(1, 12)].reshape(384, 768)
        even = lax.dot_general(low, k3[a * 3 + 1], nt, preferred_element_type=F32)
        vacc[a, :, 0] = even.reshape(12, 32, 256)
        odd = lax.dot_general(low, k3[a * 3 + 2], nt, preferred_element_type=F32)
        odd = odd + lax.dot_general(high, k3[a * 3], nt, preferred_element_type=F32)
        vacc[a, :, 1] = odd.reshape(12, 32, 256)

    def planes(ab):
        b = ab % 3
        return vs[ab // 3, pl.ds(jnp.minimum(b, 1), 12), (b + 1) % 2].reshape(384, 256)

    tn = (((0,), (0,)), ((), ()))

    def weight(ab):
        field = og3[pl.ds(0, 12)].reshape(384, 768)
        grad = lax.dot_general(planes(ab), field, tn, preferred_element_type=F32).astype(BF16)
        for c in range(3):
            ws[rows_of(FIRST_TAP + (ab * 3 + c) * 256, 256)] = grad[:, c * 256 : (c + 1) * 256]

    def b_rows(owner, j):
        return rows_of(j * B_CHUNK + owner * B_PIECE, B_PIECE)

    def sign(way):
        return 1 if way == 0 else -1

    def lanes(way):
        return pl.ds(128 * way, 128)

    def ring(way, s, j):
        piece = rows_of(j * B_PIECE, B_PIECE)
        if s == 0:
            src = ws.at[b_rows(at(dz=4)[2], j), lanes(way)]
            dst = br.at[way, 0, piece, lanes(way)]
        else:
            src, dst = br.at[way, s - 1, piece], br.at[way, s, piece]
        return remote(src, dst, brs.at[way, s, j], brr.at[way, s, j], chip(at(dz=sign(way))))

    def near(dj):
        return lax.rem(x + dj, NX)

    def ax_send(d, dz):
        xt, zt = at(dx=d)[0], at(dz=dz)[2]
        return remote(
            ws.at[rows_of(A_BASE + xt * A_BLOCK + zt * A_PIECE, A_PIECE)], rx.at[d - 1, dz],
            axs.at[d - 1, dz], axr.at[d - 1, dz], chip(at(dx=d)),
        )

    def ay_send(dy, dz):
        slot = dz * NY + dy - 1
        yt = at(dy=dy)[1]
        return remote(
            s2.at[dz, rows_of(yt * PART_A, PART_A)], ry.at[slot], ays.at[slot], ayr.at[slot],
            chip(at(dy=dy, dz=dz)),
        )

    def bx_send(dx, dy):
        slot = dx * NY + dy - 1
        xt, yt, _ = at(dx, dy)
        return remote(
            sb.at[rows_of((xt * NY + yt) * PART_B, PART_B)], bx.at[slot], bxs.at[slot], bxr.at[slot],
            chip(at(dx, dy)),
        )

    to_af[1].wait()
    vs[2, other_pairs, :, pl.ds(0, 24)] = vin[1]

    acc[...] = jnp.zeros(acc.shape, F32)

    def forward(first):
        @pl.loop(first, first + 3)
        def _(ab):
            term = jnp.dot(planes(ab), k3[ab], preferred_element_type=F32)
            for n in range(6):
                acc[n, pl.ds(8, 384)] += term[:, n * 128 : (n + 1) * 128]

    def enter(j):
        for way in range(2):
            ring(way, 0, j).start()

    def leave(xt):
        @pl.when(x != xt)
        def _():
            for dz in FAR_FIRST:
                ax_send(lax.rem(xt - x + NX, NX), dz).start()

    weight(8)
    weight(7)
    leave(3)
    weight(6)
    leave(2)
    forward(6)
    to_af[0].wait()
    vs[1, other_pairs, :, pl.ds(0, 24)] = vin[0]
    weight(5)
    leave(1)
    weight(4)
    weight(3)
    leave(0)
    forward(3)
    top_own.wait()
    top_other.wait()
    keep = jnp.where(gz > 0, 1.0, 0.0).astype(BF16)
    vs[0, own_pairs, :, pl.ds(0, 24)] = halo[0] * keep
    vs[0, other_pairs, :, pl.ds(0, 24)] = halo[1] * keep

    weight(2)
    enter(3)
    weight(1)
    enter(2)
    weight(0)
    enter(1)
    enter(0)

    for p in range(2):
        vg_af[p] = vacc[p + 1, pl.ds(6 - 6 * af, 6), :, pl.ds(0, 24)].astype(BF16)
    vg_gz[0] = vacc[0, pl.ds(6 * af, 6), :, pl.ds(0, 24)].astype(BF16)
    vg_gz[1] = vacc[0, pl.ds(6 - 6 * af, 6), :, pl.ds(0, 24)].astype(BF16)
    back_af = remote(vg_af, vin_af, es.at[4], er.at[4], dev(gz, a=1 - af))
    back_own = remote(vg_gz.at[0], vin_gz.at[0], es.at[5], er.at[5], dev(lower))
    back_other = remote(vg_gz.at[1], vin_gz.at[1], es.at[6], er.at[6], dev(lower, a=1 - af))
    for copy in (back_af, back_own, back_other):
        copy.start()

    def ring_step(s, first=0, last=NX):
        @pl.loop(first, last)
        def _(n):
            j = NX - 1 - n
            dx = lax.rem(j - x + NX, NX)
            piece = rows_of(j * B_PIECE, B_PIECE)
            for way in range(2):
                ring(way, s, j).wait_recv()
                if s == 3:
                    continue
                own = ws[b_rows(at(dz=sign(way) * (3 - s))[2], j)].astype(F32)
                if s == 0:
                    half, rest = slice(128 * way, 128 * way + 128), slice(128 - 128 * way, 256 - 128 * way)
                    br[way, 0, piece, lanes(way)] = (
                        br[way, 0, piece, lanes(way)].astype(F32) + own[:, half]
                    ).astype(BF16)
                    br[way, 0, piece, lanes(1 - way)] = own[:, rest].astype(BF16)
                else:
                    br[way, s, piece] = (br[way, s, piece].astype(F32) + own).astype(BF16)
                ring(way, s + 1, j).start()
            if s == 3:
                total = ws[b_rows(z, j)].astype(F32)
                total = total + br[0, 3, piece].astype(F32) + br[1, 3, piece].astype(F32)
                sb[piece] = total.astype(BF16)
                bx_send(dx, 1).start()

                @pl.when(dx > 0)
                def _():
                    bx_send(dx, 0).start()

    def a_piece(dz):
        zt = at(dz=dz)[2]
        total = ws[rows_of(A_BASE + x * A_BLOCK + zt * A_PIECE, A_PIECE)].astype(F32)
        for d in range(1, NX):
            ax_send(d, dz).wait_recv()
            total = total + rx[d - 1, dz].astype(F32)
        s2[dz] = total.astype(BF16)
        for dy in range(NY):
            if dy or dz:
                ay_send(dy, dz).start()

    def half(base):
        start = pl.multiple_of(base * 192, 8)
        total = None
        for c in range(3):
            term = jnp.concatenate(
                [
                    acc[c * 2 + lane, pl.ds(7 + c + start, 96, stride=2)]
                    for lane in range(2)
                ],
                axis=1,
            )
            if c == 0:
                place = lax.broadcasted_iota(jnp.int32, (96, 256), 0)
                term = jnp.where(place % 16 == 0, 0.0, term)
            total = term if total is None else total + term
        return total

    across = remote(osend, oin, es.at[7], er.at[7], dev(gz, c=1 - col))
    def finish_output():
        own_half = half(col)
        across.wait()
        out[...] = (own_half + oin[...].reshape(96, 256).astype(F32)).astype(BF16).reshape(6, 16, 256)

    def finish_gradient():
        back_af.wait()
        back_own.wait()
        back_other.wait()
        own = pl.ds(6 * af, 6)
        vg[0] = (vacc[1, own, :, pl.ds(0, 24)] + vin_af[0].astype(F32)).astype(BF16)
        above = vin_gz[0].astype(F32) + vin_gz[1].astype(F32)
        above = jnp.where(gz < count - 1, above, 0.0)
        vg[1] = (vacc[2, own, :, pl.ds(0, 24)] + vin_af[1].astype(F32) + above).astype(BF16)

    forward(0)
    osend[...] = half(1 - col).astype(BF16).reshape(6, 16, 256)
    across.start()
    a_piece(FAR_FIRST[0])
    ring_step(0)
    a_piece(FAR_FIRST[1])
    ring_step(1)
    a_piece(FAR_FIRST[2])
    a_piece(FAR_FIRST[3])
    ring_step(2)
    a_piece(FAR_FIRST[4])
    a_piece(FAR_FIRST[5])
    ring_step(3)
    finish_output()
    a_piece(FAR_FIRST[6])
    a_piece(FAR_FIRST[7])

    scale = 1.0 / jnp.sqrt(F32(9216))
    total = sb[rows_of((x * NY + y) * PART_B, PART_B)].astype(F32)
    for slot in range(XY - 1):
        bx_send((slot + 1) // NY, (slot + 1) % NY).wait_recv()
        total = total + bx[slot].astype(F32)

    def a_shard(px, py, pz):
        return rows_of(A_BASE + px * A_BLOCK + pz * A_PIECE + py * PART_A, PART_A)

    def b_shard(px, py, pz):
        return rows_of(px * B_CHUNK + pz * B_PIECE + py * PART_B, PART_B)

    full[b_shard(x, y, z)] = (total * scale).astype(BF16)

    def gbx(dx, dy, source):
        slot = dx * NY + dy - 1
        place = full.at[b_shard(*source)]
        return remote(place, place, gbxs.at[slot], gbxr.at[slot], chip(at(dx, dy)))

    def gaz(dz, source):
        place = full.at[a_shard(*source)]
        return remote(place, place, gazs.at[dz - 1], gazr.at[dz - 1], chip(at(dz=dz)))

    @pl.loop(1, XY)
    def _(t):
        gbx(t // NY, t % NY, (x, y, z)).start()

    total = s2[0, rows_of(y * PART_A, PART_A)].astype(F32)
    for dz in FAR_FIRST:
        for dy in range(NY):
            if dy or dz:
                ay_send(dy, dz).wait_recv()
                total = total + ry[dz * NY + dy - 1].astype(F32)
    full[a_shard(x, y, z)] = (total * scale).astype(BF16)

    for dz in NEAR_FIRST[1:]:
        gaz(dz, (x, y, z)).start()

    def gax(t, e, arriving=False):
        dx, dy = t // NY, t % NY
        source = at(-dx, -dy, e) if arriving else (x, y, at(dz=e)[2])
        place = full.at[a_shard(*source)]
        return remote(place, place, gaxs.at[t - 1, e], gaxr.at[t - 1, e], chip(at(dx, dy)))

    def gring(way, s, j, arriving=False):
        pz = at(dz=-sign(way) * (s + 1 if arriving else s))[2]
        place = full.at[b_rows(pz, j)] if s < 3 else full.at[b_rows(pz, j), lanes(way)]
        return remote(place, place, gbrs.at[way, s, j], gbrr.at[way, s, j], chip(at(dz=sign(way))))

    def gather_piece(e):
        if e:
            dz = NZ - e
            gaz(dz, at(dz=-dz)).wait_recv()
        for t in (4, 5, 2, 3, 6, 7, 1):
            gax(t, e).start()

    gather_piece(NEAR_FIRST[0])
    finish_gradient()

    @pl.loop(0, NX)
    def _(dj):
        j = near(dj)
        back = (NX - dj) % NX
        gbx(back, 1, at(dj, 1, 0)).wait_recv()

        @pl.when(dj > 0)
        def _():
            gbx(back, 0, at(dj, 0, 0)).wait_recv()

        for way in range(2):
            gring(way, 0, j).start()

    for s in range(4):
        for e in NEAR_FIRST[1 + 2 * s : 3 + 2 * s]:
            gather_piece(e)

        @pl.loop(0, NX)
        def _(dj):
            j = near(dj)
            for way in range(2):
                gring(way, s, j, True).wait_recv()
                if s < 3:
                    gring(way, s + 1, j).start()

    @pl.loop(0, NZ)
    def _(e):
        for t in range(1, XY):
            gax(t, e, True).wait_recv()

    @pl.loop(0, NX)
    def _(dj):
        for way in range(2):
            for s in range(4):
                ring(way, s, near(dj)).wait_send()
                gring(way, s, near(dj)).wait_send()

    @pl.loop(0, NZ)
    def _(dz):
        for d in range(1, NX):
            ax_send(d, dz).wait_send()
        for t in range(1, XY):
            gax(t, dz).wait_send()

    @pl.loop(1, YZ)
    def _(t):
        ay_send(t % NY, t // NY).wait_send()

    @pl.loop(1, NZ)
    def _(dz):
        gaz(dz, (x, y, z)).wait_send()

    @pl.loop(1, XY)
    def _(t):
        bx_send(t // NY, t % NY).wait_send()
        gbx(t // NY, t % NY, (x, y, z)).wait_send()


def on_device(volume, kernel, out_grad):
    v = volume.reshape(2, 6, 2, 24, 256)
    og = out_grad.reshape(6, 12, 256)
    k = kernel.reshape(9, 3, 256, 256)
    vmem = pl.BlockSpec(memory_space=pltpu.VMEM)
    hbm = pl.BlockSpec(memory_space=pltpu.HBM)
    dma = pltpu.SemaphoreType.DMA
    planes_shape = (2, 6, 2, 24, 256)

    def pair(*shape):
        return [dma(shape), dma(shape)]

    out, vg, kg = pl.pallas_call(
        body,
        out_shape=(
            jax.ShapeDtypeStruct((6, 16, 256), BF16),
            jax.ShapeDtypeStruct(planes_shape, BF16),
            jax.ShapeDtypeStruct((ROWS, 256), BF16),
        ),
        in_specs=[hbm, hbm, hbm],
        out_specs=(vmem, vmem, vmem),
        scratch_shapes=[
            pltpu.VMEM(planes_shape, BF16),
            pltpu.VMEM((6, 12, 256), BF16),
            pltpu.VMEM((9, 256, 768), BF16),
            pltpu.VMEM((2, 208, 128), F32),
            pltpu.VMEM((13, 32, 768), BF16),
            pltpu.VMEM((3, 13, 2, 32, 256), BF16),
            pltpu.VMEM(planes_shape, BF16),
            pltpu.VMEM(planes_shape, BF16),
            pltpu.VMEM((6, 392, 128), F32),
            pltpu.VMEM((3, 12, 2, 32, 256), F32),
            pltpu.VMEM((6, 16, 256), BF16),
            pltpu.VMEM((6, 16, 256), BF16),
            pltpu.VMEM(planes_shape, BF16),
            pltpu.VMEM(planes_shape, BF16),
            pltpu.VMEM(planes_shape, BF16),
            pltpu.VMEM(planes_shape, BF16),
            pltpu.VMEM((ROWS, 256), BF16),
            pltpu.VMEM((NX - 1, NZ, A_PIECE, 256), BF16),
            pltpu.VMEM((NZ, A_PIECE, 256), BF16),
            pltpu.VMEM((YZ - 1, PART_A, 256), BF16),
            pltpu.VMEM((2, 4, B_BLOCK, 256), BF16),
            pltpu.VMEM((B_BLOCK, 256), BF16),
            pltpu.VMEM((XY - 1, PART_B, 256), BF16),
            dma((5,)),
            *pair(9),
            *pair(NX - 1, NZ), *pair(YZ - 1), *pair(2, 4, NX), *pair(XY - 1),
            *pair(NZ - 1), *pair(XY - 1, NZ), *pair(XY - 1), *pair(2, 4, NX),
        ],
        compiler_params=pltpu.CompilerParams(
            collective_id=0, has_side_effects=True, vmem_limit_bytes=40 * 2**20
        ),
    )(*(pltpu.with_memory_space_constraint(a, pltpu.HBM) for a in (v, k, og)))
    return (
        out[:, :12].reshape(1, 6, 12, 256),
        vg.reshape(2, 12, 24, 256),
        kg[FIRST_TAP:].reshape(3, 3, 3, 256, 256),
    )


def solution(mesh):
    in_specs = (
        P("gz", "af", None, "col"),
        P(None, None, None, "col", "af"),
        P("gz", "col", None, "af"),
    )
    out_specs = (
        P("gz", "col", None, "af"),
        P("gz", "af", None, "col"),
        P(None, None, None, "col", "af"),
    )
    return jax.shard_map(
        on_device, mesh=mesh, in_specs=in_specs, out_specs=out_specs, check_vma=False
    )
```

```python
import functools

import jax
import jax.numpy as jnp
from jax import lax
from jax.experimental import pallas as pl
from jax.experimental.pallas import tpu as pltpu
from jax.sharding import PartitionSpec as P

F32 = jnp.float32
BF16 = jnp.bfloat16
MESH = pl.DeviceIdType.MESH
NX, NY, NZ = 4, 2, 8
XY, YZ = NX * NY, NY * NZ
PART_A, PART_B = 64, 48
A_BLOCK, A_PIECE = PART_A * YZ, PART_A * NY
B_BLOCK, B_PIECE = PART_B * XY, PART_B * NY
B_CHUNK = B_PIECE * NZ
A_BASE = B_BLOCK * NZ
ROWS = A_BASE + A_BLOCK * NX
FIRST_TAP = 256
FAR_FIRST = (4, 3, 5, 2, 6, 1, 7, 0)
NEAR_FIRST = (0, 1, 7, 2, 6, 3, 5, 4)


def rows_of(start, size):
    return pl.ds(pl.multiple_of(start, 16), size)


def body(
    v_hbm, k, og_hbm, out, vg, full,
    v, og, k3, up, og3, vs, vin, halo, acc, vacc, oin, osend, vg_af, vg_gz, vin_af, vin_gz,
    ws, rx, s2, ry, s3, rz, br, sb, bx,
    local_sem, es, er, axs, axr, ays, ayr, azs, azr, brs, brr, bxs, bxr,
    gazs, gazr, gaxs, gaxr, gbxs, gbxr, gbrs, gbrr,
):
    gz, col, af = lax.axis_index("gz"), lax.axis_index("col"), lax.axis_index("af")
    count = XY * NZ
    x, y, z = gz // YZ, (gz // NZ) % NY, gz % NZ
    upper, lower = lax.rem(gz + 1, count), lax.rem(gz + count - 1, count)

    def dev(g, c=col, a=af):
        return {"gz": g, "col": c, "af": a}

    def at(dx=0, dy=0, dz=0):
        return (lax.rem(x + dx + NX, NX), lax.rem(y + dy + NY, NY), lax.rem(z + dz + NZ, NZ))

    def chip(place):
        return dev((place[0] * NY + place[1]) * NZ + place[2])

    def remote(src, dst, ss, rs, target):
        return pltpu.make_async_remote_copy(
            src_ref=src, dst_ref=dst, send_sem=ss, recv_sem=rs, device_id=target, device_id_type=MESH
        )

    barrier = pltpu.get_barrier_semaphore()

    def greet(target):
        pl.semaphore_signal(barrier, inc=1, device_id=target, device_id_type=MESH)

    greet(dev(gz, c=1 - col))
    greet(dev(gz, a=1 - af))
    for g in (upper, lower):
        greet(dev(g))
        greet(dev(g, a=1 - af))

    @pl.loop(1, NZ)
    def _(dz):
        greet(chip(at(dz=dz)))

    @pl.loop(1, XY)
    def _(t):
        greet(chip(at(t // NY, t % NY, 0)))

    loads = [
        pltpu.make_async_copy(k.at[:, c], k3.at[:, :, pl.ds(c * 256, 256)], local_sem.at[c])
        for c in range(3)
    ]
    load_og = pltpu.make_async_copy(og_hbm, og, local_sem.at[3])
    load_v = pltpu.make_async_copy(v_hbm, v, local_sem.at[4])
    load_og.start()
    load_v.start()
    for load in loads:
        load.start()

    mine = pl.ds(6 * col, 6)
    up[...] = jnp.zeros(up.shape, F32)
    vs[...] = jnp.zeros(vs.shape, BF16)
    ws[pl.ds(0, FIRST_TAP)] = jnp.zeros((FIRST_TAP, 256), BF16)
    load_og.wait()
    for i in range(6):
        row = og[i].astype(F32)
        for n in range(2):
            up[n, pl.ds(8 + 32 * i, 12, stride=2)] = row[:, n * 128 : (n + 1) * 128]
    for c in range(3):
        for n in range(2):
            og3[mine, :, pl.ds(c * 256 + n * 128, 128)] = (
                up[n, pl.ds(9 - c, 192)].reshape(6, 32, 128).astype(BF16)
            )
    og3[pl.ds(12, 1)] = jnp.zeros((1, 32, 768), BF16)
    load_v.wait()
    pl.semaphore_wait(barrier, 1 + 1 + 4 + (NZ - 1) + (XY - 1))

    cot = remote(og3.at[mine], og3.at[mine], es.at[0], er.at[0], dev(gz, c=1 - col))
    to_af = [
        remote(v.at[p], vin.at[p], es.at[p + 1], er.at[p + 1], dev(gz, a=1 - af)) for p in range(2)
    ]
    top_own = remote(v.at[1], halo.at[0], es.at[8], er.at[8], dev(upper))
    top_other = remote(v.at[1], halo.at[1], es.at[3], er.at[3], dev(upper, a=1 - af))
    for copy in (cot, to_af[1], top_own):
        copy.start()

    own_pairs = pl.ds(1 + 6 * af, 6)
    other_pairs = pl.ds(7 - 6 * af, 6)
    for p in range(2):
        vs[p + 1, own_pairs, :, pl.ds(0, 24)] = v[p]

    for load in loads:
        load.wait()
    cot.wait_send()
    other = pl.ds(6 - 6 * col, 6)
    remote(og3.at[other], og3.at[other], es.at[0], er.at[0], dev(gz, c=1 - col)).wait_recv()

    nt = (((1,), (1,)), ((), ()))

    def backward(a):
        low = og3[pl.ds(0, 12)].reshape(384, 768)
        high = og3[pl.ds(1, 12)].reshape(384, 768)
        even = lax.dot_general(low, k3[a * 3 + 1], nt, preferred_element_type=F32)
        vacc[a, :, 0] = even.reshape(12, 32, 256)
        odd = lax.dot_general(low, k3[a * 3 + 2], nt, preferred_element_type=F32)
        odd = odd + lax.dot_general(high, k3[a * 3], nt, preferred_element_type=F32)
        vacc[a, :, 1] = odd.reshape(12, 32, 256)

    @pl.loop(0, 2)
    def _(a):
        backward(a)

    to_af[1].wait_send()
    to_af[0].start()
    backward(2)

    def planes(ab):
        b = ab % 3
        return vs[ab // 3, pl.ds(jnp.minimum(b, 1), 12), (b + 1) % 2].reshape(384, 256)

    tn = (((0,), (0,)), ((), ()))

    def weight(ab):
        field = og3[pl.ds(0, 12)].reshape(384, 768)
        grad = lax.dot_general(planes(ab), field, tn, preferred_element_type=F32).astype(BF16)
        for c in range(3):
            ws[rows_of(FIRST_TAP + (ab * 3 + c) * 256, 256)] = grad[:, c * 256 : (c + 1) * 256]

    def b_rows(owner, j):
        return rows_of(j * B_CHUNK + owner * B_PIECE, B_PIECE)

    def sign(way):
        return 1 if way == 0 else -1

    def lanes(way):
        return pl.ds(128 * way, 128)

    def ring(way, s, j):
        piece = rows_of(j * B_PIECE, B_PIECE)
        if s == 0:
            src = ws.at[b_rows(at(dz=4)[2], j), lanes(way)]
            dst = br.at[way, 0, piece, lanes(way)]
        else:
            src, dst = br.at[way, s - 1, piece], br.at[way, s, piece]
        return remote(src, dst, brs.at[way, s, j], brr.at[way, s, j], chip(at(dz=sign(way))))

    def near(dj):
        return lax.rem(x + dj, NX)

    def ax_send(d, dz):
        xt, zt = at(dx=d)[0], at(dz=dz)[2]
        return remote(
            ws.at[rows_of(A_BASE + xt * A_BLOCK + zt * A_PIECE, A_PIECE)], rx.at[d - 1, dz],
            axs.at[d - 1, dz], axr.at[d - 1, dz], chip(at(dx=d)),
        )

    def ay_send(dz):
        yt = at(dy=1)[1]
        return remote(
            s2.at[dz, rows_of(yt * PART_A, PART_A)], ry.at[dz], ays.at[dz], ayr.at[dz], chip(at(dy=1))
        )

    def az_send(dz):
        return remote(s3.at[dz], rz.at[dz - 1], azs.at[dz - 1], azr.at[dz - 1], chip(at(dz=dz)))

    def bx_send(dx, dy):
        slot = dx * NY + dy - 1
        xt, yt, _ = at(dx, dy)
        return remote(
            sb.at[rows_of((xt * NY + yt) * PART_B, PART_B)], bx.at[slot], bxs.at[slot], bxr.at[slot],
            chip(at(dx, dy)),
        )

    to_af[1].wait_recv()
    vs[2, other_pairs, :, pl.ds(0, 24)] = vin[1]

    acc[...] = jnp.zeros(acc.shape, F32)

    def forward(first):
        @pl.loop(first, first + 3)
        def _(ab):
            term = jnp.dot(planes(ab), k3[ab], preferred_element_type=F32)
            for n in range(6):
                acc[n, pl.ds(8, 384)] += term[:, n * 128 : (n + 1) * 128]

    def enter(j):
        for way in range(2):
            ring(way, 0, j).start()

    def leave(xt):
        @pl.when(x != xt)
        def _():
            for dz in FAR_FIRST:
                ax_send(lax.rem(xt - x + NX, NX), dz).start()

    weight(8)
    weight(7)
    leave(3)
    weight(6)
    leave(2)
    to_af[0].wait_send()
    top_other.start()
    forward(6)
    to_af[0].wait_recv()
    vs[1, other_pairs, :, pl.ds(0, 24)] = vin[0]
    weight(5)
    leave(1)
    weight(4)
    weight(3)
    leave(0)
    forward(3)
    top_own.wait()
    top_other.wait()
    keep = jnp.where(gz > 0, 1.0, 0.0).astype(BF16)
    vs[0, own_pairs, :, pl.ds(0, 24)] = halo[0] * keep
    vs[0, other_pairs, :, pl.ds(0, 24)] = halo[1] * keep

    weight(2)
    enter(3)
    weight(1)
    enter(2)
    weight(0)
    enter(1)
    enter(0)

    for p in range(2):
        vg_af[p] = vacc[p + 1, pl.ds(6 - 6 * af, 6), :, pl.ds(0, 24)].astype(BF16)
    vg_gz[0] = vacc[0, pl.ds(6 * af, 6), :, pl.ds(0, 24)].astype(BF16)
    vg_gz[1] = vacc[0, pl.ds(6 - 6 * af, 6), :, pl.ds(0, 24)].astype(BF16)
    back_af = remote(vg_af, vin_af, es.at[4], er.at[4], dev(gz, a=1 - af))
    back_own = remote(vg_gz.at[0], vin_gz.at[0], es.at[5], er.at[5], dev(lower))
    back_other = remote(vg_gz.at[1], vin_gz.at[1], es.at[6], er.at[6], dev(lower, a=1 - af))
    for copy in (back_af, back_own, back_other):
        copy.start()

    def ring_step(s, first=0, last=NX):
        @pl.loop(first, last)
        def _(n):
            j = NX - 1 - n
            dx = lax.rem(j - x + NX, NX)
            piece = rows_of(j * B_PIECE, B_PIECE)
            for way in range(2):
                ring(way, s, j).wait_recv()
                if s == 3:
                    continue
                own = ws[b_rows(at(dz=sign(way) * (3 - s))[2], j)].astype(F32)
                if s == 0:
                    half, rest = slice(128 * way, 128 * way + 128), slice(128 - 128 * way, 256 - 128 * way)
                    br[way, 0, piece, lanes(way)] = (
                        br[way, 0, piece, lanes(way)].astype(F32) + own[:, half]
                    ).astype(BF16)
                    br[way, 0, piece, lanes(1 - way)] = own[:, rest].astype(BF16)
                else:
                    br[way, s, piece] = (br[way, s, piece].astype(F32) + own).astype(BF16)
                ring(way, s + 1, j).start()
            if s == 3:
                total = ws[b_rows(z, j)].astype(F32)
                total = total + br[0, 3, piece].astype(F32) + br[1, 3, piece].astype(F32)
                sb[piece] = total.astype(BF16)
                bx_send(dx, 1).start()

                @pl.when(dx > 0)
                def _():
                    bx_send(dx, 0).start()

    def a_piece(dz):
        zt = at(dz=dz)[2]
        total = ws[rows_of(A_BASE + x * A_BLOCK + zt * A_PIECE, A_PIECE)].astype(F32)
        for d in range(1, NX):
            ax_send(d, dz).wait_recv()
            total = total + rx[d - 1, dz].astype(F32)
        s2[dz] = total.astype(BF16)
        ay_send(dz).start()

    def a_pass(dz):
        ay_send(dz).wait_recv()
        total = s2[dz, rows_of(y * PART_A, PART_A)].astype(F32) + ry[dz].astype(F32)
        s3[dz] = total.astype(BF16)
        if dz:
            az_send(dz).start()

    def half(base):
        start = pl.multiple_of(base * 192, 8)
        total = None
        for c in range(3):
            term = jnp.concatenate(
                [
                    acc[c * 2 + lane, pl.ds(7 + c + start, 96, stride=2)]
                    for lane in range(2)
                ],
                axis=1,
            )
            if c == 0:
                place = lax.broadcasted_iota(jnp.int32, (96, 256), 0)
                term = jnp.where(place % 16 == 0, 0.0, term)
            total = term if total is None else total + term
        return total

    across = remote(osend, oin, es.at[7], er.at[7], dev(gz, c=1 - col))
    def finish_output():
        own_half = half(col)
        across.wait()
        out[...] = (own_half + oin[...].reshape(96, 256).astype(F32)).astype(BF16).reshape(6, 16, 256)

    def finish_gradient():
        back_af.wait()
        back_own.wait()
        back_other.wait()
        own = pl.ds(6 * af, 6)
        vg[0] = (vacc[1, own, :, pl.ds(0, 24)] + vin_af[0].astype(F32)).astype(BF16)
        above = vin_gz[0].astype(F32) + vin_gz[1].astype(F32)
        above = jnp.where(gz < count - 1, above, 0.0)
        vg[1] = (vacc[2, own, :, pl.ds(0, 24)] + vin_af[1].astype(F32) + above).astype(BF16)

    forward(0)
    osend[...] = half(1 - col).astype(BF16).reshape(6, 16, 256)
    across.start()
    a_piece(FAR_FIRST[0])
    ring_step(0)
    a_piece(FAR_FIRST[1])
    ring_step(1)
    a_piece(FAR_FIRST[2])
    a_piece(FAR_FIRST[3])
    a_pass(FAR_FIRST[0])
    ring_step(2)
    a_piece(FAR_FIRST[4])
    a_pass(FAR_FIRST[1])
    a_piece(FAR_FIRST[5])
    a_pass(FAR_FIRST[2])
    ring_step(3)
    finish_output()
    a_piece(FAR_FIRST[6])
    a_pass(FAR_FIRST[3])
    a_piece(FAR_FIRST[7])
    a_pass(FAR_FIRST[4])
    a_pass(FAR_FIRST[5])
    a_pass(FAR_FIRST[6])
    a_pass(FAR_FIRST[7])

    scale = 1.0 / jnp.sqrt(F32(9216))
    total = sb[rows_of((x * NY + y) * PART_B, PART_B)].astype(F32)
    for slot in range(XY - 1):
        bx_send((slot + 1) // NY, (slot + 1) % NY).wait_recv()
        total = total + bx[slot].astype(F32)

    def a_shard(px, py, pz):
        return rows_of(A_BASE + px * A_BLOCK + pz * A_PIECE + py * PART_A, PART_A)

    def b_shard(px, py, pz):
        return rows_of(px * B_CHUNK + pz * B_PIECE + py * PART_B, PART_B)

    full[b_shard(x, y, z)] = (total * scale).astype(BF16)

    def gbx(dx, dy, source):
        slot = dx * NY + dy - 1
        place = full.at[b_shard(*source)]
        return remote(place, place, gbxs.at[slot], gbxr.at[slot], chip(at(dx, dy)))

    def gaz(dz, source):
        place = full.at[a_shard(*source)]
        return remote(place, place, gazs.at[dz - 1], gazr.at[dz - 1], chip(at(dz=dz)))

    @pl.loop(1, XY)
    def _(t):
        gbx(t // NY, t % NY, (x, y, z)).start()

    total = s3[0].astype(F32)
    for dz in FAR_FIRST[:-1]:
        az_send(dz).wait_recv()
        total = total + rz[dz - 1].astype(F32)
    full[a_shard(x, y, z)] = (total * scale).astype(BF16)

    for dz in NEAR_FIRST[1:]:
        gaz(dz, (x, y, z)).start()

    def gax(t, e, arriving=False):
        dx, dy = t // NY, t % NY
        source = at(-dx, -dy, e) if arriving else (x, y, at(dz=e)[2])
        place = full.at[a_shard(*source)]
        return remote(place, place, gaxs.at[t - 1, e], gaxr.at[t - 1, e], chip(at(dx, dy)))

    def gring(way, s, j, arriving=False):
        pz = at(dz=-sign(way) * (s + 1 if arriving else s))[2]
        place = full.at[b_rows(pz, j)] if s < 3 else full.at[b_rows(pz, j), lanes(way)]
        return remote(place, place, gbrs.at[way, s, j], gbrr.at[way, s, j], chip(at(dz=sign(way))))

    def gather_piece(e):
        if e:
            dz = NZ - e
            gaz(dz, at(dz=-dz)).wait_recv()
        for t in (4, 5, 2, 3, 6, 7, 1):
            gax(t, e).start()

    gather_piece(NEAR_FIRST[0])
    finish_gradient()

    @pl.loop(0, NX)
    def _(dj):
        for way in range(2):
            for s in range(4):
                ring(way, s, near(dj)).wait_send()

    @pl.loop(0, NZ)
    def _(dz):
        for d in range(1, NX):
            ax_send(d, dz).wait_send()

    @pl.loop(0, NZ)
    def _(dz):
        ay_send(dz).wait_send()

    @pl.loop(1, NZ)
    def _(dz):
        az_send(dz).wait_send()

    @pl.loop(1, XY)
    def _(t):
        bx_send(t // NY, t % NY).wait_send()

    @pl.loop(0, NX)
    def _(dj):
        j = near(dj)
        back = (NX - dj) % NX
        gbx(back, 1, at(dj, 1, 0)).wait_recv()

        @pl.when(dj > 0)
        def _():
            gbx(back, 0, at(dj, 0, 0)).wait_recv()

        for way in range(2):
            gring(way, 0, j).start()

    for s in range(4):
        for e in NEAR_FIRST[1 + 2 * s : 3 + 2 * s]:
            gather_piece(e)

        @pl.loop(0, NX)
        def _(dj):
            j = near(dj)
            for way in range(2):
                gring(way, s, j, True).wait_recv()
                if s < 3:
                    gring(way, s + 1, j).start()

    @pl.loop(0, NZ)
    def _(e):
        for t in range(1, XY):
            gax(t, e, True).wait_recv()
            gax(t, e).wait_send()

    @pl.loop(0, NX)
    def _(dj):
        for way in range(2):
            for s in range(4):
                gring(way, s, near(dj)).wait_send()

    @pl.loop(1, NZ)
    def _(dz):
        gaz(dz, (x, y, z)).wait_send()

    @pl.loop(1, XY)
    def _(t):
        gbx(t // NY, t % NY, (x, y, z)).wait_send()


def on_device(volume, kernel, out_grad):
    v = volume.reshape(2, 6, 2, 24, 256)
    og = out_grad.reshape(6, 12, 256)
    k = kernel.reshape(9, 3, 256, 256)
    vmem = pl.BlockSpec(memory_space=pltpu.VMEM)
    hbm = pl.BlockSpec(memory_space=pltpu.HBM)
    dma = pltpu.SemaphoreType.DMA
    planes_shape = (2, 6, 2, 24, 256)

    def pair(*shape):
        return [dma(shape), dma(shape)]

    out, vg, kg = pl.pallas_call(
        body,
        out_shape=(
            jax.ShapeDtypeStruct((6, 16, 256), BF16),
            jax.ShapeDtypeStruct(planes_shape, BF16),
            jax.ShapeDtypeStruct((ROWS, 256), BF16),
        ),
        in_specs=[hbm, hbm, hbm],
        out_specs=(vmem, vmem, vmem),
        scratch_shapes=[
            pltpu.VMEM(planes_shape, BF16),
            pltpu.VMEM((6, 12, 256), BF16),
            pltpu.VMEM((9, 256, 768), BF16),
            pltpu.VMEM((2, 208, 128), F32),
            pltpu.VMEM((13, 32, 768), BF16),
            pltpu.VMEM((3, 13, 2, 32, 256), BF16),
            pltpu.VMEM(planes_shape, BF16),
            pltpu.VMEM(planes_shape, BF16),
            pltpu.VMEM((6, 392, 128), F32),
            pltpu.VMEM((3, 12, 2, 32, 256), F32),
            pltpu.VMEM((6, 16, 256), BF16),
            pltpu.VMEM((6, 16, 256), BF16),
            pltpu.VMEM(planes_shape, BF16),
            pltpu.VMEM(planes_shape, BF16),
            pltpu.VMEM(planes_shape, BF16),
            pltpu.VMEM(planes_shape, BF16),
            pltpu.VMEM((ROWS, 256), BF16),
            pltpu.VMEM((NX - 1, NZ, A_PIECE, 256), BF16),
            pltpu.VMEM((NZ, A_PIECE, 256), BF16),
            pltpu.VMEM((NZ, PART_A, 256), BF16),
            pltpu.VMEM((NZ, PART_A, 256), BF16),
            pltpu.VMEM((NZ - 1, PART_A, 256), BF16),
            pltpu.VMEM((2, 4, B_BLOCK, 256), BF16),
            pltpu.VMEM((B_BLOCK, 256), BF16),
            pltpu.VMEM((XY - 1, PART_B, 256), BF16),
            dma((5,)),
            *pair(9),
            *pair(NX - 1, NZ), *pair(NZ), *pair(NZ - 1), *pair(2, 4, NX), *pair(XY - 1),
            *pair(NZ - 1), *pair(XY - 1, NZ), *pair(XY - 1), *pair(2, 4, NX),
        ],
        compiler_params=pltpu.CompilerParams(
            collective_id=0, has_side_effects=True, vmem_limit_bytes=40 * 2**20
        ),
    )(*(pltpu.with_memory_space_constraint(a, pltpu.HBM) for a in (v, k, og)))
    return (
        out[:, :12].reshape(1, 6, 12, 256),
        vg.reshape(2, 12, 24, 256),
        kg[FIRST_TAP:].reshape(3, 3, 3, 256, 256),
    )


def solution(mesh):
    in_specs = (
        P("gz", "af", None, "col"),
        P(None, None, None, "col", "af"),
        P("gz", "col", None, "af"),
    )
    out_specs = (
        P("gz", "col", None, "af"),
        P("gz", "af", None, "col"),
        P(None, None, None, "col", "af"),
    )
    return jax.shard_map(
        on_device, mesh=mesh, in_specs=in_specs, out_specs=out_specs, check_vma=False
    )
```

```python
import functools

import jax
import jax.numpy as jnp
from jax import lax
from jax.experimental import pallas as pl
from jax.experimental.pallas import tpu as pltpu
from jax.sharding import PartitionSpec as P

F32 = jnp.float32
BF16 = jnp.bfloat16
MESH = pl.DeviceIdType.MESH
NX, NY, NZ = 4, 2, 8
XY, YZ = NX * NY, NY * NZ
PART_A, PART_B = 64, 48
A_BLOCK, A_PIECE = PART_A * YZ, PART_A * NY
B_BLOCK, B_PIECE = PART_B * XY, PART_B * NY
B_CHUNK = B_PIECE * NZ
A_BASE = B_BLOCK * NZ
ROWS = A_BASE + A_BLOCK * NX
FIRST_TAP = 256
FAR_FIRST = (4, 3, 5, 2, 6, 1, 7, 0)
NEAR_FIRST = (0, 1, 7, 2, 6, 3, 5, 4)


def rows_of(start, size):
    return pl.ds(pl.multiple_of(start, 16), size)


def body(
    v_hbm, k, og_hbm, out, vg, full,
    v, og, k3, up, og3, vs, vin, halo, acc, vacc, oin, osend, vg_af, vg_gz, vin_af, vin_gz,
    ws, rx, s2, ry, s3, rz, br, sb, bx,
    local_sem, es, er, axs, axr, ays, ayr, azs, azr, brs, brr, bxs, bxr,
    gazs, gazr, gaxs, gaxr, gbxs, gbxr, gbrs, gbrr,
):
    gz, col, af = lax.axis_index("gz"), lax.axis_index("col"), lax.axis_index("af")
    count = XY * NZ
    x, y, z = gz // YZ, (gz // NZ) % NY, gz % NZ
    upper, lower = lax.rem(gz + 1, count), lax.rem(gz + count - 1, count)

    def dev(g, c=col, a=af):
        return {"gz": g, "col": c, "af": a}

    def at(dx=0, dy=0, dz=0):
        return (lax.rem(x + dx + NX, NX), lax.rem(y + dy + NY, NY), lax.rem(z + dz + NZ, NZ))

    def chip(place):
        return dev((place[0] * NY + place[1]) * NZ + place[2])

    def remote(src, dst, ss, rs, target):
        return pltpu.make_async_remote_copy(
            src_ref=src, dst_ref=dst, send_sem=ss, recv_sem=rs, device_id=target, device_id_type=MESH
        )

    barrier = pltpu.get_barrier_semaphore()

    def greet(target):
        pl.semaphore_signal(barrier, inc=1, device_id=target, device_id_type=MESH)

    greet(dev(gz, c=1 - col))
    greet(dev(gz, a=1 - af))
    for g in (upper, lower):
        greet(dev(g))
        greet(dev(g, a=1 - af))

    @pl.loop(1, NZ)
    def _(dz):
        greet(chip(at(dz=dz)))

    @pl.loop(1, XY)
    def _(t):
        greet(chip(at(t // NY, t % NY, 0)))

    loads = [
        pltpu.make_async_copy(k.at[:, c], k3.at[:, :, pl.ds(c * 256, 256)], local_sem.at[c])
        for c in range(3)
    ]
    load_og = pltpu.make_async_copy(og_hbm, og, local_sem.at[3])
    load_v = pltpu.make_async_copy(v_hbm, v, local_sem.at[4])
    load_og.start()
    load_v.start()
    for load in loads:
        load.start()

    mine = pl.ds(6 * col, 6)
    up[...] = jnp.zeros(up.shape, F32)
    vs[...] = jnp.zeros(vs.shape, BF16)
    ws[pl.ds(0, FIRST_TAP)] = jnp.zeros((FIRST_TAP, 256), BF16)
    load_og.wait()
    for i in range(6):
        row = og[i].astype(F32)
        for n in range(2):
            up[n, pl.ds(8 + 32 * i, 12, stride=2)] = row[:, n * 128 : (n + 1) * 128]
    for c in range(3):
        for n in range(2):
            og3[mine, :, pl.ds(c * 256 + n * 128, 128)] = (
                up[n, pl.ds(9 - c, 192)].reshape(6, 32, 128).astype(BF16)
            )
    og3[pl.ds(12, 1)] = jnp.zeros((1, 32, 768), BF16)
    load_v.wait()
    pl.semaphore_wait(barrier, 1 + 1 + 4 + (NZ - 1) + (XY - 1))

    cot = remote(og3.at[mine], og3.at[mine], es.at[0], er.at[0], dev(gz, c=1 - col))
    to_af = [
        remote(v.at[p], vin.at[p], es.at[p + 1], er.at[p + 1], dev(gz, a=1 - af)) for p in range(2)
    ]
    top_own = remote(v.at[1], halo.at[0], es.at[8], er.at[8], dev(upper))
    top_other = remote(v.at[1], halo.at[1], es.at[3], er.at[3], dev(upper, a=1 - af))
    for copy in (cot, to_af[1], top_own):
        copy.start()

    own_pairs = pl.ds(1 + 6 * af, 6)
    other_pairs = pl.ds(7 - 6 * af, 6)
    for p in range(2):
        vs[p + 1, own_pairs, :, pl.ds(0, 24)] = v[p]

    for load in loads:
        load.wait()
    cot.wait_send()
    other = pl.ds(6 - 6 * col, 6)
    remote(og3.at[other], og3.at[other], es.at[0], er.at[0], dev(gz, c=1 - col)).wait_recv()

    nt = (((1,), (1,)), ((), ()))

    def backward(a):
        low = og3[pl.ds(0, 12)].reshape(384, 768)
        high = og3[pl.ds(1, 12)].reshape(384, 768)
        even = lax.dot_general(low, k3[a * 3 + 1], nt, preferred_element_type=F32)
        vacc[a, :, 0] = even.reshape(12, 32, 256)
        odd = lax.dot_general(low, k3[a * 3 + 2], nt, preferred_element_type=F32)
        odd = odd + lax.dot_general(high, k3[a * 3], nt, preferred_element_type=F32)
        vacc[a, :, 1] = odd.reshape(12, 32, 256)

    @pl.loop(0, 2)
    def _(a):
        backward(a)

    to_af[1].wait_send()
    to_af[0].start()
    backward(2)

    def planes(ab):
        b = ab % 3
        return vs[ab // 3, pl.ds(jnp.minimum(b, 1), 12), (b + 1) % 2].reshape(384, 256)

    tn = (((0,), (0,)), ((), ()))

    def weight(ab):
        field = og3[pl.ds(0, 12)].reshape(384, 768)
        grad = lax.dot_general(planes(ab), field, tn, preferred_element_type=F32).astype(BF16)
        for c in range(3):
            ws[rows_of(FIRST_TAP + (ab * 3 + c) * 256, 256)] = grad[:, c * 256 : (c + 1) * 256]

    def b_rows(owner, j):
        return rows_of(j * B_CHUNK + owner * B_PIECE, B_PIECE)

    def sign(way):
        return 1 if way == 0 else -1

    def lanes(way):
        return pl.ds(128 * way, 128)

    def ring(way, s, j):
        piece = rows_of(j * B_PIECE, B_PIECE)
        if s == 0:
            src = ws.at[b_rows(at(dz=4)[2], j), lanes(way)]
            dst = br.at[way, 0, piece, lanes(way)]
        else:
            src, dst = br.at[way, s - 1, piece], br.at[way, s, piece]
        return remote(src, dst, brs.at[way, s, j], brr.at[way, s, j], chip(at(dz=sign(way))))

    def near(dj):
        return lax.rem(x + dj, NX)

    def ax_send(d, dz):
        xt, zt = at(dx=d)[0], at(dz=dz)[2]
        return remote(
            ws.at[rows_of(A_BASE + xt * A_BLOCK + zt * A_PIECE, A_PIECE)], rx.at[d - 1, dz],
            axs.at[d - 1, dz], axr.at[d - 1, dz], chip(at(dx=d)),
        )

    def ay_send(dz):
        yt = at(dy=1)[1]
        return remote(
            s2.at[dz, rows_of(yt * PART_A, PART_A)], ry.at[dz], ays.at[dz], ayr.at[dz], chip(at(dy=1))
        )

    def az_send(dz):
        return remote(s3.at[dz], rz.at[dz - 1], azs.at[dz - 1], azr.at[dz - 1], chip(at(dz=dz)))

    def bx_send(dx, dy):
        slot = dx * NY + dy - 1
        xt, yt, _ = at(dx, dy)
        return remote(
            sb.at[rows_of((xt * NY + yt) * PART_B, PART_B)], bx.at[slot], bxs.at[slot], bxr.at[slot],
            chip(at(dx, dy)),
        )

    to_af[1].wait_recv()
    vs[2, other_pairs, :, pl.ds(0, 24)] = vin[1]

    acc[...] = jnp.zeros(acc.shape, F32)

    def forward(first):
        @pl.loop(first, first + 3)
        def _(ab):
            term = jnp.dot(planes(ab), k3[ab], preferred_element_type=F32)
            for n in range(6):
                acc[n, pl.ds(8, 384)] += term[:, n * 128 : (n + 1) * 128]

    def enter(j):
        for way in range(2):
            ring(way, 0, j).start()

    def leave(xt):
        @pl.when(x != xt)
        def _():
            for dz in FAR_FIRST:
                ax_send(lax.rem(xt - x + NX, NX), dz).start()

    weight(8)
    weight(7)
    leave(3)
    weight(6)
    leave(2)
    to_af[0].wait_send()
    top_other.start()
    forward(6)
    to_af[0].wait_recv()
    vs[1, other_pairs, :, pl.ds(0, 24)] = vin[0]
    weight(5)
    leave(1)
    weight(4)
    weight(3)
    leave(0)
    forward(3)
    top_own.wait()
    top_other.wait()
    keep = jnp.where(gz > 0, 1.0, 0.0).astype(BF16)
    vs[0, own_pairs, :, pl.ds(0, 24)] = halo[0] * keep
    vs[0, other_pairs, :, pl.ds(0, 24)] = halo[1] * keep

    weight(2)
    enter(3)
    weight(1)
    enter(2)
    weight(0)
    enter(1)
    enter(0)

    for p in range(2):
        vg_af[p] = vacc[p + 1, pl.ds(6 - 6 * af, 6), :, pl.ds(0, 24)].astype(BF16)
    vg_gz[0] = vacc[0, pl.ds(6 * af, 6), :, pl.ds(0, 24)].astype(BF16)
    vg_gz[1] = vacc[0, pl.ds(6 - 6 * af, 6), :, pl.ds(0, 24)].astype(BF16)
    back_af = remote(vg_af, vin_af, es.at[4], er.at[4], dev(gz, a=1 - af))
    back_own = remote(vg_gz.at[0], vin_gz.at[0], es.at[5], er.at[5], dev(lower))
    back_other = remote(vg_gz.at[1], vin_gz.at[1], es.at[6], er.at[6], dev(lower, a=1 - af))
    for copy in (back_af, back_own, back_other):
        copy.start()

    def ring_step(s, first=0, last=NX):
        @pl.loop(first, last)
        def _(n):
            j = NX - 1 - n
            dx = lax.rem(j - x + NX, NX)
            piece = rows_of(j * B_PIECE, B_PIECE)
            for way in range(2):
                ring(way, s, j).wait_recv()
                if s == 3:
                    continue
                own = ws[b_rows(at(dz=sign(way) * (3 - s))[2], j)].astype(F32)
                if s == 0:
                    half, rest = slice(128 * way, 128 * way + 128), slice(128 - 128 * way, 256 - 128 * way)
                    br[way, 0, piece, lanes(way)] = (
                        br[way, 0, piece, lanes(way)].astype(F32) + own[:, half]
                    ).astype(BF16)
                    br[way, 0, piece, lanes(1 - way)] = own[:, rest].astype(BF16)
                else:
                    br[way, s, piece] = (br[way, s, piece].astype(F32) + own).astype(BF16)
                ring(way, s + 1, j).start()
            if s == 3:
                total = ws[b_rows(z, j)].astype(F32)
                total = total + br[0, 3, piece].astype(F32) + br[1, 3, piece].astype(F32)
                sb[piece] = total.astype(BF16)
                bx_send(dx, 1).start()

                @pl.when(dx > 0)
                def _():
                    bx_send(dx, 0).start()

    def a_piece(dz):
        zt = at(dz=dz)[2]
        total = ws[rows_of(A_BASE + x * A_BLOCK + zt * A_PIECE, A_PIECE)].astype(F32)
        for d in range(1, NX):
            ax_send(d, dz).wait_recv()
            total = total + rx[d - 1, dz].astype(F32)
        s2[dz] = total.astype(BF16)
        ay_send(dz).start()

    def a_pass(dz):
        ay_send(dz).wait_recv()
        total = s2[dz, rows_of(y * PART_A, PART_A)].astype(F32) + ry[dz].astype(F32)
        s3[dz] = total.astype(BF16)
        if dz:
            az_send(dz).start()

    def half(base):
        start = pl.multiple_of(base * 192, 8)
        total = None
        for c in range(3):
            term = jnp.concatenate(
                [
                    acc[c * 2 + lane, pl.ds(7 + c + start, 96, stride=2)]
                    for lane in range(2)
                ],
                axis=1,
            )
            if c == 0:
                place = lax.broadcasted_iota(jnp.int32, (96, 256), 0)
                term = jnp.where(place % 16 == 0, 0.0, term)
            total = term if total is None else total + term
        return total

    across = remote(osend, oin, es.at[7], er.at[7], dev(gz, c=1 - col))
    def finish_output():
        own_half = half(col)
        across.wait()
        out[...] = (own_half + oin[...].reshape(96, 256).astype(F32)).astype(BF16).reshape(6, 16, 256)

    def finish_gradient():
        back_af.wait()
        back_own.wait()
        back_other.wait()
        own = pl.ds(6 * af, 6)
        vg[0] = (vacc[1, own, :, pl.ds(0, 24)] + vin_af[0].astype(F32)).astype(BF16)
        above = vin_gz[0].astype(F32) + vin_gz[1].astype(F32)
        above = jnp.where(gz < count - 1, above, 0.0)
        vg[1] = (vacc[2, own, :, pl.ds(0, 24)] + vin_af[1].astype(F32) + above).astype(BF16)

    forward(0)
    osend[...] = half(1 - col).astype(BF16).reshape(6, 16, 256)
    across.start()
    a_piece(FAR_FIRST[0])
    ring_step(0)
    a_piece(FAR_FIRST[1])
    ring_step(1)
    a_piece(FAR_FIRST[2])
    a_piece(FAR_FIRST[3])
    a_pass(FAR_FIRST[0])
    ring_step(2)
    a_piece(FAR_FIRST[4])
    a_pass(FAR_FIRST[1])
    a_piece(FAR_FIRST[5])
    a_pass(FAR_FIRST[2])
    ring_step(3)
    finish_output()
    a_piece(FAR_FIRST[6])
    a_pass(FAR_FIRST[3])
    a_piece(FAR_FIRST[7])
    a_pass(FAR_FIRST[4])
    a_pass(FAR_FIRST[5])
    a_pass(FAR_FIRST[6])
    a_pass(FAR_FIRST[7])

    scale = 1.0 / jnp.sqrt(F32(9216))
    total = sb[rows_of((x * NY + y) * PART_B, PART_B)].astype(F32)
    for slot in range(XY - 1):
        bx_send((slot + 1) // NY, (slot + 1) % NY).wait_recv()
        total = total + bx[slot].astype(F32)

    def a_shard(px, py, pz):
        return rows_of(A_BASE + px * A_BLOCK + pz * A_PIECE + py * PART_A, PART_A)

    def b_shard(px, py, pz):
        return rows_of(px * B_CHUNK + pz * B_PIECE + py * PART_B, PART_B)

    full[b_shard(x, y, z)] = (total * scale).astype(BF16)

    def gbx(dx, dy, source):
        slot = dx * NY + dy - 1
        place = full.at[b_shard(*source)]
        return remote(place, place, gbxs.at[slot], gbxr.at[slot], chip(at(dx, dy)))

    def gaz(dz, source):
        place = full.at[a_shard(*source)]
        return remote(place, place, gazs.at[dz - 1], gazr.at[dz - 1], chip(at(dz=dz)))

    @pl.loop(1, XY)
    def _(t):
        gbx(t // NY, t % NY, (x, y, z)).start()

    total = s3[0].astype(F32)
    for dz in FAR_FIRST[:-1]:
        az_send(dz).wait_recv()
        total = total + rz[dz - 1].astype(F32)
    full[a_shard(x, y, z)] = (total * scale).astype(BF16)

    for dz in NEAR_FIRST[1:]:
        gaz(dz, (x, y, z)).start()

    def gax(t, e, arriving=False):
        dx, dy = t // NY, t % NY
        source = at(-dx, -dy, e) if arriving else (x, y, at(dz=e)[2])
        place = full.at[a_shard(*source)]
        return remote(place, place, gaxs.at[t - 1, e], gaxr.at[t - 1, e], chip(at(dx, dy)))

    def gring(way, s, j, arriving=False):
        pz = at(dz=-sign(way) * (s + 1 if arriving else s))[2]
        place = full.at[b_rows(pz, j)] if s < 3 else full.at[b_rows(pz, j), lanes(way)]
        return remote(place, place, gbrs.at[way, s, j], gbrr.at[way, s, j], chip(at(dz=sign(way))))

    def gather_piece(e):
        if e:
            dz = NZ - e
            gaz(dz, at(dz=-dz)).wait_recv()
        for t in (4, 5, 2, 3, 6, 7, 1):
            gax(t, e).start()

    gather_piece(NEAR_FIRST[0])
    finish_gradient()

    @pl.loop(0, NX)
    def _(dj):
        for way in range(2):
            for s in range(4):
                ring(way, s, near(dj)).wait_send()

    @pl.loop(0, NZ)
    def _(dz):
        for d in range(1, NX):
            ax_send(d, dz).wait_send()

    @pl.loop(0, NZ)
    def _(dz):
        ay_send(dz).wait_send()

    @pl.loop(1, NZ)
    def _(dz):
        az_send(dz).wait_send()

    @pl.loop(1, XY)
    def _(t):
        bx_send(t // NY, t % NY).wait_send()

    @pl.loop(0, NX)
    def _(dj):
        j = near(dj)
        back = (NX - dj) % NX
        gbx(back, 1, at(dj, 1, 0)).wait_recv()

        @pl.when(dj > 0)
        def _():
            gbx(back, 0, at(dj, 0, 0)).wait_recv()

        for way in range(2):
            gring(way, 0, j).start()

    for s in range(4):
        for e in NEAR_FIRST[(1, 4, 7, 8)[s] : (4, 7, 8, 8)[s]]:
            gather_piece(e)

        @pl.loop(0, NX)
        def _(dj):
            j = near(dj)
            for way in range(2):
                gring(way, s, j, True).wait_recv()
                if s < 3:
                    gring(way, s + 1, j).start()

    @pl.loop(0, NZ)
    def _(e):
        for t in range(1, XY):
            gax(t, e, True).wait_recv()
            gax(t, e).wait_send()

    @pl.loop(0, NX)
    def _(dj):
        for way in range(2):
            for s in range(4):
                gring(way, s, near(dj)).wait_send()

    @pl.loop(1, NZ)
    def _(dz):
        gaz(dz, (x, y, z)).wait_send()

    @pl.loop(1, XY)
    def _(t):
        gbx(t // NY, t % NY, (x, y, z)).wait_send()


def on_device(volume, kernel, out_grad):
    v = volume.reshape(2, 6, 2, 24, 256)
    og = out_grad.reshape(6, 12, 256)
    k = kernel.reshape(9, 3, 256, 256)
    vmem = pl.BlockSpec(memory_space=pltpu.VMEM)
    hbm = pl.BlockSpec(memory_space=pltpu.HBM)
    dma = pltpu.SemaphoreType.DMA
    planes_shape = (2, 6, 2, 24, 256)

    def pair(*shape):
        return [dma(shape), dma(shape)]

    out, vg, kg = pl.pallas_call(
        body,
        out_shape=(
            jax.ShapeDtypeStruct((6, 16, 256), BF16),
            jax.ShapeDtypeStruct(planes_shape, BF16),
            jax.ShapeDtypeStruct((ROWS, 256), BF16),
        ),
        in_specs=[hbm, hbm, hbm],
        out_specs=(vmem, vmem, vmem),
        scratch_shapes=[
            pltpu.VMEM(planes_shape, BF16),
            pltpu.VMEM((6, 12, 256), BF16),
            pltpu.VMEM((9, 256, 768), BF16),
            pltpu.VMEM((2, 208, 128), F32),
            pltpu.VMEM((13, 32, 768), BF16),
            pltpu.VMEM((3, 13, 2, 32, 256), BF16),
            pltpu.VMEM(planes_shape, BF16),
            pltpu.VMEM(planes_shape, BF16),
            pltpu.VMEM((6, 392, 128), F32),
            pltpu.VMEM((3, 12, 2, 32, 256), F32),
            pltpu.VMEM((6, 16, 256), BF16),
            pltpu.VMEM((6, 16, 256), BF16),
            pltpu.VMEM(planes_shape, BF16),
            pltpu.VMEM(planes_shape, BF16),
            pltpu.VMEM(planes_shape, BF16),
            pltpu.VMEM(planes_shape, BF16),
            pltpu.VMEM((ROWS, 256), BF16),
            pltpu.VMEM((NX - 1, NZ, A_PIECE, 256), BF16),
            pltpu.VMEM((NZ, A_PIECE, 256), BF16),
            pltpu.VMEM((NZ, PART_A, 256), BF16),
            pltpu.VMEM((NZ, PART_A, 256), BF16),
            pltpu.VMEM((NZ - 1, PART_A, 256), BF16),
            pltpu.VMEM((2, 4, B_BLOCK, 256), BF16),
            pltpu.VMEM((B_BLOCK, 256), BF16),
            pltpu.VMEM((XY - 1, PART_B, 256), BF16),
            dma((5,)),
            *pair(9),
            *pair(NX - 1, NZ), *pair(NZ), *pair(NZ - 1), *pair(2, 4, NX), *pair(XY - 1),
            *pair(NZ - 1), *pair(XY - 1, NZ), *pair(XY - 1), *pair(2, 4, NX),
        ],
        compiler_params=pltpu.CompilerParams(
            collective_id=0, has_side_effects=True, vmem_limit_bytes=40 * 2**20
        ),
    )(*(pltpu.with_memory_space_constraint(a, pltpu.HBM) for a in (v, k, og)))
    return (
        out[:, :12].reshape(1, 6, 12, 256),
        vg.reshape(2, 12, 24, 256),
        kg[FIRST_TAP:].reshape(3, 3, 3, 256, 256),
    )


def solution(mesh):
    in_specs = (
        P("gz", "af", None, "col"),
        P(None, None, None, "col", "af"),
        P("gz", "col", None, "af"),
    )
    out_specs = (
        P("gz", "col", None, "af"),
        P("gz", "af", None, "col"),
        P(None, None, None, "col", "af"),
    )
    return jax.shard_map(
        on_device, mesh=mesh, in_specs=in_specs, out_specs=out_specs, check_vma=False
    )
```
